32 devices in a mesh: ka: 8 (over y, x, core), ga: 4 (over z).
Axes of the slice: x: 2, y: 2, z: 4, core: 2. Of those that a mesh axis runs over, the one named last changes fastest.
Arguments:
- band_coefs: bfloat16 [8, 16, 2, 2048], P('ka'), may hold values from -12 to 12
- screening: bfloat16 [1, 2048, 2048], P(None, 'ga'), may hold values from -0.125 to 0.125
- grid_index: int32 [2048], replicated, may hold values from 1 to 4095, as said below
Outputs:
- kernel: float32 [8, 1, 64, 128], P('ka', None, 'ga')
The draws below stay inside these ranges and needn't reach their ends.
Inputs may be any that keep to these rules, and one draw needn't show every extreme that they name: `grid_index`: the 2048 values are distinct flat grid indices x * 16 * 16 + y * 16 + z; the anchor 0 never appears.
All inputs are finite; a program needn't handle non-finite values.
Results may differ from the reference program's by a relative error of at most 0.0049.
Values may be sent and summed in bfloat16 or wider, within the bound.
A program may use at most 64 MiB of HBM per device.

```python
import math
import jax
import jax.numpy as jnp
from jax import lax

NBND = 8
NG = 2048
NFFT = 16
NS = 1
NK = 8
GRID = 4096


def draw_grid_index(key, part):
    inner = jax.random.permutation(key, GRID - 3)[:NG - 2] + 2
    chosen = jnp.concatenate([inner.astype(jnp.int32), jnp.array([1, GRID - 1], jnp.int32)])
    order = jax.random.permutation(jax.random.fold_in(key, 7), NG)
    return chosen[order].astype(jnp.int32)


def level_of(own_key, shape, split, least, largest):
    loudness = 1.0
    for dim, blocks in split:
        heights = jax.random.uniform(jax.random.fold_in(jax.random.fold_in(own_key, 6), dim), (blocks,), jnp.float32, least / len(split), largest / len(split))
        loudness = loudness * jnp.repeat(jnp.exp(heights), shape[dim] // blocks).reshape((-1,) + (1,) * (len(shape) - 1 - dim))
    return loudness


def bell_draw(key, shape, width, reach, pieces=(), kind=jnp.bfloat16):
    level = level_of(key, shape, pieces, -0.22, 0.18) if pieces else 1.0
    drawn = jax.random.normal(key, shape, jnp.float32) * width * level
    return jnp.minimum(jnp.maximum(drawn, -reach), reach).astype(kind)


def setup_inputs(seed: int = 0) -> dict:
    arg_keys = jax.random.split(jax.random.key(seed), 4)
    band_coefs = bell_draw(arg_keys[0], (NK, 2 * NBND, 2, NG), 2.0, 12.0, ((0, 8),))
    screening = bell_draw(arg_keys[1], (NS, NG, NG), NG ** -0.5, 0.125, ((1, 4),))
    grid_index = draw_grid_index(jax.random.fold_in(arg_keys[3], 71), 0)
    return dict(band_coefs=band_coefs, screening=screening, grid_index=grid_index)


def orbitals(bands, grid_index):
    values = bands.astype(jnp.float32)
    flat = jnp.zeros((bands.shape[0], 2, GRID), jnp.float32).at[:, :, grid_index].set(values)
    field = (flat[:, 0] + 1j * flat[:, 1]).reshape(bands.shape[0], NFFT, NFFT, NFFT)
    return jnp.fft.ifftn(field, axes=(1, 2, 3), norm='ortho')

def densities(first, second, grid_index):
    product = jnp.conj(first)[:, None] * second[None, :]
    product = product.reshape(first.shape[0] * second.shape[0], NFFT, NFFT, NFFT)
    spectrum = jnp.fft.fftn(product, axes=(1, 2, 3), norm='ortho').reshape(product.shape[0], GRID)
    picked = spectrum[:, grid_index]
    return jnp.stack([jnp.real(picked), jnp.imag(picked)], axis=1).astype(jnp.bfloat16)

def reference(band_coefs, screening, grid_index):
    pair_count = NBND * NBND
    scale = 1.0 / math.sqrt(NG)
    blocks = []
    for offset in range(NS):

        def one_point(point):
            here = orbitals(lax.dynamic_index_in_dim(band_coefs, point, 0, False), grid_index)
            other = ((point - offset - 1) % NK).astype(jnp.int32)
            there = orbitals(lax.dynamic_index_in_dim(band_coefs, other, 0, False), grid_index)
            return (densities(here[:NBND], there[:NBND], grid_index), densities(here[NBND:], there[NBND:], grid_index))
        valence, conduction = lax.map(one_point, jnp.arange(NK, dtype=jnp.int32))
        mixed = jnp.dot(valence.reshape(NK * 2 * pair_count, NG), screening[offset].T, preferred_element_type=jnp.float32)
        screened = mixed.astype(jnp.bfloat16).reshape(NK, pair_count, 2, NG)

        def contract(inputs):
            cond, scr = inputs
            left = cond.reshape(pair_count, 2 * NG)
            right_real = scr.reshape(pair_count, 2 * NG)
            right_imag = jnp.concatenate([scr[:, 1], -scr[:, 0]], axis=1)
            real_part = jnp.dot(left, right_real.T, preferred_element_type=jnp.float32)
            imag_part = jnp.dot(left, right_imag.T, preferred_element_type=jnp.float32)
            return jnp.concatenate([real_part, imag_part], axis=1) * scale
        blocks.append(lax.map(contract, (conduction, screened)))
    return jnp.stack(blocks, axis=1)
```

```python
import functools
import math

import jax
import jax.numpy as jnp
import numpy as np
from jax import lax
from jax.experimental import pallas as pl
from jax.experimental.pallas import tpu as pltpu
from jax.sharding import PartitionSpec as P

NBND = 8
NFFT = 16
PLANE = NFFT * NFFT
GRID = NFFT * PLANE
PAIRS = NBND * NBND
LANES = 2 * PAIRS
BANDS = 4 * NBND
BF = jnp.bfloat16
F32 = jnp.float32
MESH = pl.DeviceIdType.MESH


def radix4(parts, sign):
    (ar, ai), (br, bi), (cr, ci), (dr, di) = parts
    sr, si = ar + cr, ai + ci
    tr, ti = ar - cr, ai - ci
    ur, ui = br + dr, bi + di
    vr, vi = br - dr, bi - di
    first = (sr + ur, si + ui)
    third = (sr - ur, si - ui)
    plus = (tr - vi, ti + vr)
    minus = (tr + vi, ti - vr)
    if sign > 0:
        return [first, plus, third, minus]
    return [first, minus, third, plus]


def twiddle(value, power, sign):
    re, im = value
    power = (power * (1 if sign > 0 else -1)) % 16
    if power == 0:
        return value
    if power == 4:
        return (-im, re)
    if power == 12:
        return (im, -re)
    cosine = math.cos(2.0 * math.pi * power / 16)
    sine = math.sin(2.0 * math.pi * power / 16)
    if power % 4 == 2:
        half = math.sqrt(0.5)
        p = 1.0 if cosine > 0 else -1.0
        q = 1.0 if sine > 0 else -1.0
        if p == q:
            return ((re - im) * (p * half), (re + im) * (p * half))
        return ((re + im) * (p * half), (im - re) * (p * half))
    return (re * cosine - im * sine, re * sine + im * cosine)


def fft16(values, sign):
    inner = [radix4([values[4 * j + i] for j in range(4)], sign) for i in range(4)]
    out = [None] * 16
    for k1 in range(4):
        parts = [twiddle(inner[i][k1], i * k1, sign) for i in range(4)]
        for k2, got in enumerate(radix4(parts, sign)):
            out[k1 + 4 * k2] = got
    return out


def tables():
    group = np.arange(LANES) // BANDS
    band = np.arange(LANES) % BANDS
    same = (band[:, None] == band[None, :]).astype(np.float64)
    mats = []
    for k1 in range(4):
        angle = 2.0 * np.pi * (group[:, None] * (k1 + 4 * group[None, :]) % 16) / 16
        c, s = np.cos(angle) * same, np.sin(angle) * same
        mats.append(np.block([[c, s], [-s, c]]))
    full = np.stack(mats).astype(np.float32)
    high = full.astype(BF)
    low = (full - high.astype(np.float32)).astype(BF)
    lane = np.arange(LANES)
    kind, pair = lane // PAIRS, lane % PAIRS
    first = kind * NBND + pair // NBND
    second = 2 * NBND + kind * NBND + pair % NBND
    spread = []
    for g in range(4):
        here = (group == g)[:, None]
        block = np.concatenate(
            [here & (band[:, None] == first[None, :]), here & (band[:, None] == second[None, :])], axis=1
        )
        spread.append(np.concatenate([block, block], axis=0) * 0.125)
    return high, low, np.stack(spread).astype(BF)


def split(value):
    high = value.astype(BF)
    return high, (value - high.astype(F32)).astype(BF)


def compute(strip, rows, here_ref, there_ref, vec_ref, idx_ref, w_ref, mh_ref, ml_ref, e_ref, out_ref,
            pre, pim, qre, qim, vgrid, cgrid, vpick, cpick):
    waves = vec_ref.shape[1]
    index = vec_ref[...]
    cut_x = index // PLANE
    cut_n = index % PLANE
    points = lax.broadcasted_iota(jnp.int32, (PLANE, waves), 0)
    onehot = jnp.where(points == cut_n, 1.0 / 64, 0.0).astype(BF)
    coefs = [
        jnp.concatenate([here_ref[:, c, :], there_ref[:, c, :]], axis=0) for c in range(2)
    ]
    for j in range(4):
        masks = [(cut_x == 4 * j + i).astype(F32).astype(BF) for i in range(4)]
        block = jnp.concatenate([coefs[c] * masks[i] for c in range(2) for i in range(4)], axis=0)
        field = lax.dot_general(onehot, block, (((1,), (1,)), ((), ())), preferred_element_type=F32)
        pre[pl.ds(j * PLANE, PLANE), :] = field[:, :LANES]
        pim[pl.ds(j * PLANE, PLANE), :] = field[:, LANES:]

    @pl.loop(0, 8)
    def _(step):
        base = (step // 2) * PLANE + (step % 2) * 8
        at = [pl.ds(pl.multiple_of(base + y * NFFT, 8), 8) for y in range(NFFT)]
        for y, (re, im) in enumerate(fft16([(pre[a, :], pim[a, :]) for a in at], 1)):
            pre[at[y], :] = re
            pim[at[y], :] = im

    @pl.loop(0, 8)
    def _(step):
        base = pl.multiple_of(step * 128, 128)
        got = fft16(
            [(pre[pl.ds(base + z, 8, stride=NFFT), :], pim[pl.ds(base + z, 8, stride=NFFT), :]) for z in range(NFFT)], 1
        )
        for z, (re, im) in enumerate(got):
            pre[pl.ds(base + z * 8, 8), :] = re
            pim[pl.ds(base + z * 8, 8), :] = im

    quarters = [(pre[pl.ds(j * PLANE, PLANE), :], pim[pl.ds(j * PLANE, PLANE), :]) for j in range(4)]
    for k1, (re, im) in enumerate(radix4(quarters, 1)):
        high, low = split(jnp.concatenate([re, im], axis=1))
        mixed = (
            jnp.dot(high, mh_ref[k1], preferred_element_type=F32)
            + jnp.dot(low, mh_ref[k1], preferred_element_type=F32)
            + jnp.dot(high, ml_ref[k1], preferred_element_type=F32)
        )
        left_re = jnp.concatenate(split(mixed[:, :LANES]), axis=1)
        left_im = jnp.concatenate(split(mixed[:, LANES:]), axis=1)
        for g in range(4):
            real = jnp.dot(left_re, e_ref[g], preferred_element_type=F32)
            imag = jnp.dot(left_im, e_ref[g], preferred_element_type=F32)
            ar, br = real[:, :LANES], real[:, LANES:]
            ai, bi = imag[:, :LANES], imag[:, LANES:]
            at = pl.ds((k1 + 4 * g) * PLANE, PLANE)
            qre[at, :] = ar * br + ai * bi
            qim[at, :] = ar * bi - ai * br

    @pl.loop(0, 32)
    def _(step):
        at = [pl.ds(pl.multiple_of(x * PLANE + step * 8, 8), 8) for x in range(NFFT)]
        for x, (re, im) in enumerate(fft16([(qre[a, :], qim[a, :]) for a in at], -1)):
            qre[at[x], :] = re
            qim[at[x], :] = im

    @pl.loop(0, 32)
    def _(step):
        at = [pl.ds(pl.multiple_of(step * 128 + z * 8, 8), 8) for z in range(NFFT)]
        for z, (re, im) in enumerate(fft16([(qre[a, :], qim[a, :]) for a in at], -1)):
            qre[at[z], :] = re
            qim[at[z], :] = im

    left_half = lax.broadcasted_iota(jnp.int32, (8, LANES), 1) < PAIRS

    @pl.loop(0, 32)
    def _(step):
        plane = (step // 2) * PLANE
        half = step % 2
        take = [
            pl.ds(plane + (y // 8) * 128 + half * 64 + y % 8, 8, stride=8) for y in range(NFFT)
        ]
        for y, (re, im) in enumerate(fft16([(qre[a, :], qim[a, :]) for a in take], -1)):
            at = pl.ds(pl.multiple_of(plane + y * NFFT + half * 8, 8), 8)
            vgrid[at, :] = jnp.where(left_half, re, pltpu.roll(im, PAIRS, 1))
            cgrid[at, :] = jnp.where(left_half, pltpu.roll(re, PAIRS, 1), im)

    @pl.loop(0, waves // 32)
    def _(step):
        for u in range(32):
            g = step * 32 + u
            vpick[pl.ds(g, 1), :] = vgrid[pl.ds(idx_ref[g], 1), :]

    start = lax.axis_index("ga") * strip

    @pl.loop(0, strip // 32)
    def _(step):
        for u in range(32):
            g = step * 32 + u
            cpick[pl.ds(g, 1), :] = cgrid[pl.ds(idx_ref[start + g], 1), :]

    screened = jnp.dot(w_ref[...], vpick[...].astype(BF), preferred_element_type=F32).astype(BF)
    left = cpick[...].T.astype(BF)
    cross = jnp.dot(left, screened, preferred_element_type=F32)
    top, bottom = cross[:PAIRS], pltpu.roll(cross[PAIRS:], PAIRS, 1)
    lane = lax.broadcasted_iota(jnp.int32, (PAIRS, LANES), 1)
    total = jnp.where(lane < PAIRS, top + bottom, top - bottom) * (1.0 / math.sqrt(waves))
    for d in range(PAIRS // rows):
        out_ref[d] = total[d * rows:(d + 1) * rows]


def scatter_sum(width, x_ref, out_ref, slots, send_sem, recv_sem):
    me = lax.axis_index("ga")
    barrier = pltpu.get_barrier_semaphore()
    for step in range(1, width):
        pl.semaphore_signal(barrier, inc=1, device_id={"ga": lax.rem(me + step, width)}, device_id_type=MESH)
    pl.semaphore_wait(barrier, width - 1)
    copies = []
    for step in range(1, width):
        peer = lax.rem(me + step, width)
        copy = pltpu.make_async_remote_copy(
            src_ref=x_ref.at[peer],
            dst_ref=slots.at[step - 1],
            send_sem=send_sem.at[step - 1],
            recv_sem=recv_sem.at[step - 1],
            device_id={"ga": peer},
            device_id_type=MESH,
        )
        copy.start()
        copies.append(copy)
    total = x_ref[me]
    for step, copy in enumerate(copies):
        copy.wait_recv()
        total = total + slots[step]
    out_ref[...] = total
    for copy in copies:
        copy.wait_send()


def body(band_coefs, screening, grid_index):
    width = lax.axis_size("ga")
    count = lax.axis_size("ka")
    strip, waves = screening.shape[1:]
    rows = PAIRS // width
    here = band_coefs[0]
    there = lax.ppermute(here, "ka", [(i, (i + 1) % count) for i in range(count)])
    high, low, spread = tables()
    vmem = pl.BlockSpec(memory_space=pltpu.VMEM)
    smem = pl.BlockSpec(memory_space=pltpu.SMEM)
    terms = pl.pallas_call(
        functools.partial(compute, strip, rows),
        out_shape=jax.ShapeDtypeStruct((width, rows, LANES), F32),
        in_specs=[vmem, vmem, vmem, smem, vmem, vmem, vmem, vmem],
        out_specs=vmem,
        scratch_shapes=[
            pltpu.VMEM((4 * PLANE, LANES), F32),
            pltpu.VMEM((4 * PLANE, LANES), F32),
            pltpu.VMEM((GRID, LANES), F32),
            pltpu.VMEM((GRID, LANES), F32),
            pltpu.VMEM((GRID, LANES), F32),
            pltpu.VMEM((GRID, LANES), F32),
            pltpu.VMEM((waves, LANES), F32),
            pltpu.VMEM((strip, LANES), F32),
        ],
        compiler_params=pltpu.CompilerParams(vmem_limit_bytes=48 * 1024 * 1024),
    )(here, there, grid_index[None], grid_index, screening[0], jnp.asarray(high), jnp.asarray(low), jnp.asarray(spread))
    result = pl.pallas_call(
        functools.partial(scatter_sum, width),
        out_shape=jax.ShapeDtypeStruct((rows, LANES), F32),
        in_specs=[vmem],
        out_specs=vmem,
        scratch_shapes=[
            pltpu.VMEM((width - 1, rows, LANES), F32),
            pltpu.SemaphoreType.DMA((width - 1,)),
            pltpu.SemaphoreType.DMA((width - 1,)),
        ],
        compiler_params=pltpu.CompilerParams(collective_id=0, has_side_effects=True),
    )(terms)
    return result[None, None]


def solution(mesh):
    return jax.shard_map(
        body,
        mesh=mesh,
        in_specs=(P("ka", None, None, None), P(None, "ga", None), P()),
        out_specs=P("ka", None, "ga", None),
        check_vma=False,
    )
```

```python
import functools
import math

import jax
import jax.numpy as jnp
import numpy as np
from jax import lax
from jax.experimental import pallas as pl
from jax.experimental.pallas import tpu as pltpu
from jax.sharding import PartitionSpec as P

NBND = 8
NFFT = 16
PLANE = NFFT * NFFT
GRID = NFFT * PLANE
PAIRS = NBND * NBND
LANES = 2 * PAIRS
BANDS = 4 * NBND
BF = jnp.bfloat16
F32 = jnp.float32
MESH = pl.DeviceIdType.MESH


def radix4(parts, sign):
    (ar, ai), (br, bi), (cr, ci), (dr, di) = parts
    sr, si = ar + cr, ai + ci
    tr, ti = ar - cr, ai - ci
    ur, ui = br + dr, bi + di
    vr, vi = br - dr, bi - di
    first = (sr + ur, si + ui)
    third = (sr - ur, si - ui)
    plus = (tr - vi, ti + vr)
    minus = (tr + vi, ti - vr)
    if sign > 0:
        return [first, plus, third, minus]
    return [first, minus, third, plus]


def twiddle(value, power, sign):
    re, im = value
    power = (power * (1 if sign > 0 else -1)) % 16
    if power == 0:
        return value
    if power == 4:
        return (-im, re)
    if power == 12:
        return (im, -re)
    cosine = math.cos(2.0 * math.pi * power / 16)
    sine = math.sin(2.0 * math.pi * power / 16)
    if power % 4 == 2:
        half = math.sqrt(0.5)
        p = 1.0 if cosine > 0 else -1.0
        q = 1.0 if sine > 0 else -1.0
        if p == q:
            return ((re - im) * (p * half), (re + im) * (p * half))
        return ((re + im) * (p * half), (im - re) * (p * half))
    return (re * cosine - im * sine, re * sine + im * cosine)


def fft16(values, sign):
    inner = [radix4([values[4 * j + i] for j in range(4)], sign) for i in range(4)]
    out = [None] * 16
    for k1 in range(4):
        parts = [twiddle(inner[i][k1], i * k1, sign) for i in range(4)]
        for k2, got in enumerate(radix4(parts, sign)):
            out[k1 + 4 * k2] = got
    return out


def tables():
    half = BANDS // 2
    group = np.arange(LANES) // half % 4
    band = np.arange(LANES) // PAIRS * half + np.arange(LANES) % half
    same = (band[:, None] == band[None, :]).astype(np.float64)
    mats = []
    for k1 in range(4):
        angle = 2.0 * np.pi * (group[:, None] * (k1 + 4 * group[None, :]) % 16) / 16
        c, s = np.cos(angle) * same, np.sin(angle) * same
        mats.append(np.block([[c, s], [-s, c]]))
    full = np.stack(mats).astype(np.float32)
    high = full.astype(BF)
    low = (full - high.astype(np.float32)).astype(BF)
    lane = np.arange(LANES)
    kind, pair = lane // PAIRS, lane % PAIRS
    first = kind * NBND + pair // NBND
    second = 2 * NBND + kind * NBND + pair % NBND
    spread = []
    for g in range(4):
        here = (group == g)[:, None]
        block = np.concatenate(
            [here & (band[:, None] == first[None, :]), here & (band[:, None] == second[None, :])], axis=1
        )
        spread.append(np.concatenate([block, block], axis=0) * 0.125)
    return high, low, np.stack(spread).astype(BF)


def split(value):
    high = value.astype(BF)
    return high, (value - high.astype(F32)).astype(BF)


def scattered(coef_ref, cut_x, onehot, first):
    parts = [coef_ref[:, c, :] for c in range(2)]
    block = []
    for j in (first, first + 1):
        masks = [(cut_x == 4 * j + i).astype(F32).astype(BF) for i in range(4)]
        block += [parts[c] * masks[i] for c in range(2) for i in range(4)]
    block = jnp.concatenate(block, axis=0)
    return lax.dot_general(onehot, block, (((1,), (1,)), ((), ())), preferred_element_type=F32)


def compute(width, count, strip, rows, coef_hbm, vec_hbm, idx_hbm, w_hbm, mh_hbm, ml_hbm, e_hbm, out_ref,
            here_ref, there_ref, vec_ref, idx_ref, w_ref, mh_ref, ml_ref, e_ref,
            own, pre, pim, qre, qim, vgrid, cgrid, vpick, cpick, blocks, slots,
            in_sem, ring_send, ring_recv, send_sem, recv_sem):
    me = lax.axis_index("ga")
    point = lax.axis_index("ka")
    pairs = [(vec_hbm, vec_ref), (coef_hbm, here_ref), (idx_hbm, idx_ref), (mh_hbm, mh_ref), (ml_hbm, ml_ref),
             (e_hbm, e_ref), (w_hbm, w_ref)]
    fetch = [pltpu.make_async_copy(src, dst, in_sem.at[n]) for n, (src, dst) in enumerate(pairs)]
    for copy in fetch:
        copy.start()
    barrier = pltpu.get_barrier_semaphore()
    left_point = lax.rem(point + count - 1, count)
    pl.semaphore_signal(barrier, inc=1, device_id={"ka": left_point}, device_id_type=MESH)
    for step in range(1, width):
        pl.semaphore_signal(barrier, inc=1, device_id={"ga": lax.rem(me + step, width)}, device_id_type=MESH)
    pl.semaphore_wait(barrier, width)
    ring = pltpu.make_async_remote_copy(
        src_ref=coef_hbm,
        dst_ref=there_ref,
        send_sem=ring_send,
        recv_sem=ring_recv,
        device_id={"ka": lax.rem(point + 1, count)},
        device_id_type=MESH,
    )
    ring.start()
    fetch[0].wait()
    fetch[1].wait()
    waves = vec_ref.shape[1]
    index = vec_ref[...]
    cut_x = index // PLANE
    cut_n = index % PLANE
    points = lax.broadcasted_iota(jnp.int32, (PLANE, waves), 0)
    onehot = jnp.where(points == cut_n, 1.0 / 64, 0.0).astype(BF)
    for j in (0, 2):
        own[:, pl.ds(j * LANES, 2 * LANES)] = scattered(here_ref, cut_x, onehot, j)
    ring.wait()
    lower = lax.broadcasted_iota(jnp.int32, (PLANE, LANES), 1) < PAIRS
    for j in (0, 2):
        other = scattered(there_ref, cut_x, onehot, j)
        for e in range(2):
            mine = own[:, pl.ds((j + e) * LANES, LANES)]
            far = other[:, e * LANES:(e + 1) * LANES]
            pre[pl.ds((j + e) * PLANE, PLANE), :] = jnp.where(lower, mine, pltpu.roll(far, PAIRS, 1))
            pim[pl.ds((j + e) * PLANE, PLANE), :] = jnp.where(lower, pltpu.roll(mine, PAIRS, 1), far)

    @pl.loop(0, 8)
    def _(step):
        base = (step // 2) * PLANE + (step % 2) * 8
        at = [pl.ds(pl.multiple_of(base + y * NFFT, 8), 8) for y in range(NFFT)]
        for y, (re, im) in enumerate(fft16([(pre[a, :], pim[a, :]) for a in at], 1)):
            pre[at[y], :] = re
            pim[at[y], :] = im

    @pl.loop(0, 8)
    def _(step):
        base = pl.multiple_of(step * 128, 128)
        got = fft16(
            [(pre[pl.ds(base + z, 8, stride=NFFT), :], pim[pl.ds(base + z, 8, stride=NFFT), :]) for z in range(NFFT)], 1
        )
        for z, (re, im) in enumerate(got):
            pre[pl.ds(base + z * 8, 8), :] = re
            pim[pl.ds(base + z * 8, 8), :] = im

    for copy in fetch[2:]:
        copy.wait()
    quarters = [(pre[pl.ds(j * PLANE, PLANE), :], pim[pl.ds(j * PLANE, PLANE), :]) for j in range(4)]
    for k1, (re, im) in enumerate(radix4(quarters, 1)):
        high, low = split(jnp.concatenate([re, im], axis=1))
        mixed = (
            jnp.dot(high, mh_ref[k1], preferred_element_type=F32)
            + jnp.dot(low, mh_ref[k1], preferred_element_type=F32)
            + jnp.dot(high, ml_ref[k1], preferred_element_type=F32)
        )
        left_re = jnp.concatenate(split(mixed[:, :LANES]), axis=1)
        left_im = jnp.concatenate(split(mixed[:, LANES:]), axis=1)
        for g in range(4):
            real = jnp.dot(left_re, e_ref[g], preferred_element_type=F32)
            imag = jnp.dot(left_im, e_ref[g], preferred_element_type=F32)
            ar, br = real[:, :LANES], real[:, LANES:]
            ai, bi = imag[:, :LANES], imag[:, LANES:]
            at = pl.ds((k1 + 4 * g) * PLANE, PLANE)
            qre[at, :] = ar * br + ai * bi
            qim[at, :] = ar * bi - ai * br

    @pl.loop(0, 32)
    def _(step):
        at = [pl.ds(pl.multiple_of(x * PLANE + step * 8, 8), 8) for x in range(NFFT)]
        for x, (re, im) in enumerate(fft16([(qre[a, :], qim[a, :]) for a in at], -1)):
            qre[at[x], :] = re
            qim[at[x], :] = im

    @pl.loop(0, 32)
    def _(step):
        at = [pl.ds(pl.multiple_of(step * 128 + z * 8, 8), 8) for z in range(NFFT)]
        for z, (re, im) in enumerate(fft16([(qre[a, :], qim[a, :]) for a in at], -1)):
            qre[at[z], :] = re
            qim[at[z], :] = im

    left_half = lax.broadcasted_iota(jnp.int32, (8, LANES), 1) < PAIRS

    @pl.loop(0, 32)
    def _(step):
        plane = (step // 2) * PLANE
        half = step % 2
        take = [
            pl.ds(plane + (y // 8) * 128 + half * 64 + y % 8, 8, stride=8) for y in range(NFFT)
        ]
        for y, (re, im) in enumerate(fft16([(qre[a, :], qim[a, :]) for a in take], -1)):
            at = pl.ds(pl.multiple_of(plane + y * NFFT + half * 8, 8), 8)
            vgrid[at, :] = jnp.where(left_half, re, pltpu.roll(im, PAIRS, 1))
            cgrid[at, :] = jnp.where(left_half, pltpu.roll(re, PAIRS, 1), im)

    @pl.loop(0, waves // 32)
    def _(step):
        for u in range(32):
            g = step * 32 + u
            vpick[pl.ds(g, 1), :] = vgrid[pl.ds(idx_ref[g], 1), :]

    start = me * strip

    @pl.loop(0, strip // 32)
    def _(step):
        for u in range(32):
            g = step * 32 + u
            cpick[pl.ds(g, 1), :] = cgrid[pl.ds(idx_ref[start + g], 1), :]

    screened = jnp.dot(w_ref[...], vpick[...].astype(BF), preferred_element_type=F32).astype(BF)
    left = cpick[...].T.astype(BF)
    cross = jnp.dot(left, screened, preferred_element_type=F32)
    top, bottom = cross[:PAIRS], pltpu.roll(cross[PAIRS:], PAIRS, 1)
    lane = lax.broadcasted_iota(jnp.int32, (PAIRS, LANES), 1)
    total = jnp.where(lane < PAIRS, top + bottom, top - bottom)
    for d in range(width):
        blocks[d] = total[d * rows:(d + 1) * rows]
    copies = []
    for step in range(1, width):
        peer = lax.rem(me + step, width)
        copy = pltpu.make_async_remote_copy(
            src_ref=blocks.at[peer],
            dst_ref=slots.at[step - 1],
            send_sem=send_sem.at[step - 1],
            recv_sem=recv_sem.at[step - 1],
            device_id={"ga": peer},
            device_id_type=MESH,
        )
        copy.start()
        copies.append(copy)
    total = blocks[me]
    for step, copy in enumerate(copies):
        copy.wait_recv()
        total = total + slots[step]
    out_ref[...] = total
    for copy in copies:
        copy.wait_send()


def body(band_coefs, screening, grid_index):
    width = lax.axis_size("ga")
    count = lax.axis_size("ka")
    strip, waves = screening.shape[1:]
    rows = PAIRS // width
    here = band_coefs[0]
    high, low, spread = (jnp.asarray(t) for t in tables())
    hbm = pl.BlockSpec(memory_space=pltpu.HBM)
    result = pl.pallas_call(
        functools.partial(compute, width, count, strip, rows),
        out_shape=jax.ShapeDtypeStruct((rows, LANES), F32),
        in_specs=[hbm] * 7,
        out_specs=pl.BlockSpec(memory_space=pltpu.VMEM),
        scratch_shapes=[
            pltpu.VMEM(here.shape, BF),
            pltpu.VMEM(here.shape, BF),
            pltpu.VMEM((1, waves), jnp.int32),
            pltpu.SMEM((waves,), jnp.int32),
            pltpu.VMEM((strip, waves), BF),
            pltpu.VMEM(high.shape, BF),
            pltpu.VMEM(low.shape, BF),
            pltpu.VMEM(spread.shape, BF),
            pltpu.VMEM((PLANE, 4 * LANES), F32),
            pltpu.VMEM((4 * PLANE, LANES), F32),
            pltpu.VMEM((4 * PLANE, LANES), F32),
            pltpu.VMEM((GRID, LANES), F32),
            pltpu.VMEM((GRID, LANES), F32),
            pltpu.VMEM((GRID, LANES), F32),
            pltpu.VMEM((GRID, LANES), F32),
            pltpu.VMEM((waves, LANES), F32),
            pltpu.VMEM((strip, LANES), F32),
            pltpu.VMEM((width, rows, LANES), F32),
            pltpu.VMEM((width - 1, rows, LANES), F32),
            pltpu.SemaphoreType.DMA((7,)),
            pltpu.SemaphoreType.DMA,
            pltpu.SemaphoreType.DMA,
            pltpu.SemaphoreType.DMA((width - 1,)),
            pltpu.SemaphoreType.DMA((width - 1,)),
        ],
        compiler_params=pltpu.CompilerParams(
            collective_id=0, has_side_effects=True, vmem_limit_bytes=56 * 1024 * 1024
        ),
    )(here, grid_index[None], grid_index, screening[0], high, low, spread)
    return (result * (1.0 / math.sqrt(waves)))[None, None]


def solution(mesh):
    return jax.shard_map(
        body,
        mesh=mesh,
        in_specs=(P("ka", None, None, None), P(None, "ga", None), P()),
        out_specs=P("ka", None, "ga", None),
        check_vma=False,
    )
```

```python
import functools
import math

import jax
import jax.numpy as jnp
import numpy as np
from jax import lax
from jax.experimental import pallas as pl
from jax.experimental.pallas import tpu as pltpu
from jax.sharding import PartitionSpec as P

NBND = 8
NFFT = 16
PLANE = NFFT * NFFT
GRID = NFFT * PLANE
PAIRS = NBND * NBND
LANES = 2 * PAIRS
BANDS = 4 * NBND
BF = jnp.bfloat16
F32 = jnp.float32
MESH = pl.DeviceIdType.MESH


def radix4(parts, sign):
    (ar, ai), (br, bi), (cr, ci), (dr, di) = parts
    sr, si = ar + cr, ai + ci
    tr, ti = ar - cr, ai - ci
    ur, ui = br + dr, bi + di
    vr, vi = br - dr, bi - di
    first = (sr + ur, si + ui)
    third = (sr - ur, si - ui)
    plus = (tr - vi, ti + vr)
    minus = (tr + vi, ti - vr)
    if sign > 0:
        return [first, plus, third, minus]
    return [first, minus, third, plus]


def twiddle(value, power, sign):
    re, im = value
    power = (power * (1 if sign > 0 else -1)) % 16
    if power == 0:
        return value
    if power == 4:
        return (-im, re)
    if power == 12:
        return (im, -re)
    cosine = math.cos(2.0 * math.pi * power / 16)
    sine = math.sin(2.0 * math.pi * power / 16)
    if power % 4 == 2:
        half = math.sqrt(0.5)
        p = 1.0 if cosine > 0 else -1.0
        q = 1.0 if sine > 0 else -1.0
        if p == q:
            return ((re - im) * (p * half), (re + im) * (p * half))
        return ((re + im) * (p * half), (im - re) * (p * half))
    return (re * cosine - im * sine, re * sine + im * cosine)


def fft16(values, sign):
    inner = [radix4([values[4 * j + i] for j in range(4)], sign) for i in range(4)]
    out = [None] * 16
    for k1 in range(4):
        parts = [twiddle(inner[i][k1], i * k1, sign) for i in range(4)]
        for k2, got in enumerate(radix4(parts, sign)):
            out[k1 + 4 * k2] = got
    return out


def tables():
    half = BANDS // 2
    group = np.arange(LANES) // half % 4
    band = np.arange(LANES) // PAIRS * half + np.arange(LANES) % half
    same = (band[:, None] == band[None, :]).astype(np.float64)
    mats = []
    for k1 in range(4):
        angle = 2.0 * np.pi * (group[:, None] * (k1 + 4 * group[None, :]) % 16) / 16
        c, s = np.cos(angle) * same, np.sin(angle) * same
        mats.append(np.block([[c, s], [-s, c]]))
    full = np.stack(mats).astype(np.float32)
    high = full.astype(BF)
    low = (full - high.astype(np.float32)).astype(BF)
    lane = np.arange(LANES)
    kind, pair = lane // PAIRS, lane % PAIRS
    first = kind * NBND + pair // NBND
    second = 2 * NBND + kind * NBND + pair % NBND
    spread = []
    for g in range(4):
        here = (group == g)[:, None]
        block = np.concatenate(
            [here & (band[:, None] == first[None, :]), here & (band[:, None] == second[None, :])], axis=1
        )
        spread.append(np.concatenate([block, block], axis=0) * 0.125)
    return high, low, np.stack(spread).astype(BF)


def split(value):
    high = value.astype(BF)
    return high, (value - high.astype(F32)).astype(BF)


def scattered(coef_ref, cut_x, onehot, first):
    parts = [coef_ref[:, c, :] for c in range(2)]
    block = []
    for j in (first, first + 1):
        masks = [(cut_x == 4 * j + i).astype(F32).astype(BF) for i in range(4)]
        block += [parts[c] * masks[i] for c in range(2) for i in range(4)]
    block = jnp.concatenate(block, axis=0)
    return lax.dot_general(onehot, block, (((1,), (1,)), ((), ())), preferred_element_type=F32)


def compute(width, count, strip, rows, coef_hbm, vec_hbm, idx_hbm, w_hbm, mh_hbm, ml_hbm, e_hbm, out_ref,
            here_ref, there_ref, vec_ref, idx_ref, w_ref, mh_ref, ml_ref, e_ref,
            own, pre, pim, qre, qim, vgrid, cgrid, vpick, cpick, blocks, slots,
            in_sem, ring_send, ring_recv, send_sem, recv_sem):
    me = lax.axis_index("ga")
    point = lax.axis_index("ka")
    pairs = [(vec_hbm, vec_ref), (coef_hbm, here_ref), (idx_hbm, idx_ref), (mh_hbm, mh_ref), (ml_hbm, ml_ref),
             (e_hbm, e_ref), (w_hbm, w_ref)]
    fetch = [pltpu.make_async_copy(src, dst, in_sem.at[n]) for n, (src, dst) in enumerate(pairs)]
    for copy in fetch:
        copy.start()
    barrier = pltpu.get_barrier_semaphore()
    left_point = lax.rem(point + count - 1, count)
    pl.semaphore_signal(barrier, inc=1, device_id={"ka": left_point}, device_id_type=MESH)
    for step in range(1, width):
        pl.semaphore_signal(barrier, inc=1, device_id={"ga": lax.rem(me + step, width)}, device_id_type=MESH)
    pl.semaphore_wait(barrier, width)
    ring = pltpu.make_async_remote_copy(
        src_ref=coef_hbm,
        dst_ref=there_ref,
        send_sem=ring_send,
        recv_sem=ring_recv,
        device_id={"ka": lax.rem(point + 1, count)},
        device_id_type=MESH,
    )
    ring.start()
    fetch[0].wait()
    fetch[1].wait()
    waves = vec_ref.shape[1]
    index = vec_ref[...]
    cut_x = index // PLANE
    cut_n = index % PLANE
    points = lax.broadcasted_iota(jnp.int32, (PLANE, waves), 0)
    onehot = jnp.where(points == cut_n, 1.0 / 64, 0.0).astype(BF)
    for j in (0, 2):
        own[:, pl.ds(j * LANES, 2 * LANES)] = scattered(here_ref, cut_x, onehot, j)
    ring.wait()
    lower = lax.broadcasted_iota(jnp.int32, (PLANE, LANES), 1) < PAIRS
    for j in (0, 2):
        other = scattered(there_ref, cut_x, onehot, j)
        for e in range(2):
            mine = own[:, pl.ds((j + e) * LANES, LANES)]
            far = other[:, e * LANES:(e + 1) * LANES]
            pre[pl.ds((j + e) * PLANE, PLANE), :] = jnp.where(lower, mine, pltpu.roll(far, PAIRS, 1))
            pim[pl.ds((j + e) * PLANE, PLANE), :] = jnp.where(lower, pltpu.roll(mine, PAIRS, 1), far)

    @pl.loop(0, 8, unroll=4)
    def _(step):
        base = (step // 2) * PLANE + (step % 2) * 8
        at = [pl.ds(pl.multiple_of(base + y * NFFT, 8), 8) for y in range(NFFT)]
        for y, (re, im) in enumerate(fft16([(pre[a, :], pim[a, :]) for a in at], 1)):
            qre[at[y], :] = re
            qim[at[y], :] = im

    @pl.loop(0, 8, unroll=4)
    def _(step):
        base = pl.multiple_of(step * 128, 128)
        got = fft16(
            [(qre[pl.ds(base + z, 8, stride=NFFT), :], qim[pl.ds(base + z, 8, stride=NFFT), :]) for z in range(NFFT)], 1
        )
        for z, (re, im) in enumerate(got):
            pre[pl.ds(base + z * 8, 8), :] = re
            pim[pl.ds(base + z * 8, 8), :] = im

    for copy in fetch[2:]:
        copy.wait()
    quarters = [(pre[pl.ds(j * PLANE, PLANE), :], pim[pl.ds(j * PLANE, PLANE), :]) for j in range(4)]
    for k1, (re, im) in enumerate(radix4(quarters, 1)):
        high, low = split(jnp.concatenate([re, im], axis=1))
        mixed = (
            jnp.dot(high, mh_ref[k1], preferred_element_type=F32)
            + jnp.dot(low, mh_ref[k1], preferred_element_type=F32)
            + jnp.dot(high, ml_ref[k1], preferred_element_type=F32)
        )
        both = jnp.concatenate([mixed[:, :LANES], mixed[:, LANES:]], axis=0)
        lines = jnp.concatenate(split(both), axis=1)
        for g in range(4):
            field = jnp.dot(lines, e_ref[g], preferred_element_type=F32)
            ar, br = field[:PLANE, :LANES], field[:PLANE, LANES:]
            ai, bi = field[PLANE:, :LANES], field[PLANE:, LANES:]
            at = pl.ds((k1 + 4 * g) * PLANE, PLANE)
            qre[at, :] = ar * br + ai * bi
            qim[at, :] = ar * bi - ai * br

    @pl.loop(0, 32, unroll=4)
    def _(step):
        at = [pl.ds(pl.multiple_of(x * PLANE + step * 8, 8), 8) for x in range(NFFT)]
        for x, (re, im) in enumerate(fft16([(qre[a, :], qim[a, :]) for a in at], -1)):
            vgrid[at[x], :] = re
            cgrid[at[x], :] = im

    @pl.loop(0, 32, unroll=4)
    def _(step):
        at = [pl.ds(pl.multiple_of(step * 128 + z * 8, 8), 8) for z in range(NFFT)]
        for z, (re, im) in enumerate(fft16([(vgrid[a, :], cgrid[a, :]) for a in at], -1)):
            qre[at[z], :] = re
            qim[at[z], :] = im

    left_half = lax.broadcasted_iota(jnp.int32, (8, LANES), 1) < PAIRS

    @pl.loop(0, 32, unroll=4)
    def _(step):
        plane = (step // 2) * PLANE
        half = step % 2
        take = [
            pl.ds(plane + (y // 8) * 128 + half * 64 + y % 8, 8, stride=8) for y in range(NFFT)
        ]
        for y, (re, im) in enumerate(fft16([(qre[a, :], qim[a, :]) for a in take], -1)):
            at = pl.ds(pl.multiple_of(plane + y * NFFT + half * 8, 8), 8)
            vgrid[at, :] = jnp.where(left_half, re, pltpu.roll(im, PAIRS, 1))
            cgrid[at, :] = jnp.where(left_half, pltpu.roll(re, PAIRS, 1), im)

    @pl.loop(0, waves // 32)
    def _(step):
        base = pl.multiple_of(step * 32, 32)
        for u in range(32):
            g = base + u
            vpick[pl.ds(g, 1), :] = vgrid[pl.ds(idx_ref[g], 1), :]

    start = me * strip

    @pl.loop(0, strip // 32)
    def _(step):
        base = pl.multiple_of(step * 32, 32)
        for u in range(32):
            g = base + u
            cpick[pl.ds(g, 1), :] = cgrid[pl.ds(idx_ref[start + g], 1), :]

    screened = jnp.dot(w_ref[...], vpick[...].astype(BF), preferred_element_type=F32).astype(BF)
    left = cpick[...].T.astype(BF)
    cross = jnp.dot(left, screened, preferred_element_type=F32)
    top, bottom = cross[:PAIRS], pltpu.roll(cross[PAIRS:], PAIRS, 1)
    lane = lax.broadcasted_iota(jnp.int32, (PAIRS, LANES), 1)
    total = jnp.where(lane < PAIRS, top + bottom, top - bottom)
    for d in range(width):
        blocks[d] = total[d * rows:(d + 1) * rows]
    copies = []
    for step in range(1, width):
        peer = lax.rem(me + step, width)
        copy = pltpu.make_async_remote_copy(
            src_ref=blocks.at[peer],
            dst_ref=slots.at[step - 1],
            send_sem=send_sem.at[step - 1],
            recv_sem=recv_sem.at[step - 1],
            device_id={"ga": peer},
            device_id_type=MESH,
        )
        copy.start()
        copies.append(copy)
    total = blocks[me]
    for step, copy in enumerate(copies):
        copy.wait_recv()
        total = total + slots[step]
    out_ref[...] = total
    for copy in copies:
        copy.wait_send()


def body(band_coefs, screening, grid_index):
    width = lax.axis_size("ga")
    count = lax.axis_size("ka")
    strip, waves = screening.shape[1:]
    rows = PAIRS // width
    here = band_coefs[0]
    high, low, spread = (jnp.asarray(t) for t in tables())
    hbm = pl.BlockSpec(memory_space=pltpu.HBM)
    result = pl.pallas_call(
        functools.partial(compute, width, count, strip, rows),
        out_shape=jax.ShapeDtypeStruct((rows, LANES), F32),
        in_specs=[hbm] * 7,
        out_specs=pl.BlockSpec(memory_space=pltpu.VMEM),
        scratch_shapes=[
            pltpu.VMEM(here.shape, BF),
            pltpu.VMEM(here.shape, BF),
            pltpu.VMEM((1, waves), jnp.int32),
            pltpu.SMEM((waves,), jnp.int32),
            pltpu.VMEM((strip, waves), BF),
            pltpu.VMEM(high.shape, BF),
            pltpu.VMEM(low.shape, BF),
            pltpu.VMEM(spread.shape, BF),
            pltpu.VMEM((PLANE, 4 * LANES), F32),
            pltpu.VMEM((4 * PLANE, LANES), F32),
            pltpu.VMEM((4 * PLANE, LANES), F32),
            pltpu.VMEM((GRID, LANES), F32),
            pltpu.VMEM((GRID, LANES), F32),
            pltpu.VMEM((GRID, LANES), F32),
            pltpu.VMEM((GRID, LANES), F32),
            pltpu.VMEM((waves, LANES), F32),
            pltpu.VMEM((strip, LANES), F32),
            pltpu.VMEM((width, rows, LANES), F32),
            pltpu.VMEM((width - 1, rows, LANES), F32),
            pltpu.SemaphoreType.DMA((7,)),
            pltpu.SemaphoreType.DMA,
            pltpu.SemaphoreType.DMA,
            pltpu.SemaphoreType.DMA((width - 1,)),
            pltpu.SemaphoreType.DMA((width - 1,)),
        ],
        compiler_params=pltpu.CompilerParams(
            collective_id=0, has_side_effects=True, vmem_limit_bytes=56 * 1024 * 1024
        ),
    )(here, grid_index[None], grid_index, screening[0], high, low, spread)
    return (result * (1.0 / math.sqrt(waves)))[None, None]


def solution(mesh):
    return jax.shard_map(
        body,
        mesh=mesh,
        in_specs=(P("ka", None, None, None), P(None, "ga", None), P()),
        out_specs=P("ka", None, "ga", None),
        check_vma=False,
    )
```

```python
import functools
import math

import jax
import jax.numpy as jnp
import numpy as np
from jax import lax
from jax.experimental import pallas as pl
from jax.experimental.pallas import tpu as pltpu
from jax.sharding import PartitionSpec as P

NBND = 8
NFFT = 16
PLANE = NFFT * NFFT
GRID = NFFT * PLANE
PAIRS = NBND * NBND
LANES = 2 * PAIRS
BANDS = 4 * NBND
BF = jnp.bfloat16
F32 = jnp.float32
MESH = pl.DeviceIdType.MESH


def radix4(parts, sign):
    (ar, ai), (br, bi), (cr, ci), (dr, di) = parts
    sr, si = ar + cr, ai + ci
    tr, ti = ar - cr, ai - ci
    ur, ui = br + dr, bi + di
    vr, vi = br - dr, bi - di
    first = (sr + ur, si + ui)
    third = (sr - ur, si - ui)
    plus = (tr - vi, ti + vr)
    minus = (tr + vi, ti - vr)
    if sign > 0:
        return [first, plus, third, minus]
    return [first, minus, third, plus]


def twiddle(value, power, sign):
    re, im = value
    power = (power * (1 if sign > 0 else -1)) % 16
    if power == 0:
        return value
    if power == 4:
        return (-im, re)
    if power == 12:
        return (im, -re)
    cosine = math.cos(2.0 * math.pi * power / 16)
    sine = math.sin(2.0 * math.pi * power / 16)
    if power % 4 == 2:
        half = math.sqrt(0.5)
        p = 1.0 if cosine > 0 else -1.0
        q = 1.0 if sine > 0 else -1.0
        if p == q:
            return ((re - im) * (p * half), (re + im) * (p * half))
        return ((re + im) * (p * half), (im - re) * (p * half))
    return (re * cosine - im * sine, re * sine + im * cosine)


def fft16(values, sign):
    inner = [radix4([values[4 * j + i] for j in range(4)], sign) for i in range(4)]
    out = [None] * 16
    for k1 in range(4):
        parts = [twiddle(inner[i][k1], i * k1, sign) for i in range(4)]
        for k2, got in enumerate(radix4(parts, sign)):
            out[k1 + 4 * k2] = got
    return out


def tables():
    half = BANDS // 2
    group = np.arange(LANES) // half
    band = np.arange(LANES) % half
    same = (band[:, None] == band[None, :]).astype(np.float64)
    mats = []
    for k1 in range(2):
        angle = 2.0 * np.pi * (group[:, None] * (k1 + 2 * group[None, :]) % 16) / 16
        c, s = np.cos(angle) * same, np.sin(angle) * same
        mats.append(np.block([[c, s], [-s, c]]))
    full = np.stack(mats).astype(np.float32)
    high = full.astype(BF)
    low = (full - high.astype(np.float32)).astype(BF)
    lane = np.arange(LANES)
    kind, pair = lane // PAIRS, lane % PAIRS
    spread = []
    for wanted in (kind * NBND + pair // NBND, kind * NBND + pair % NBND):
        for g in range(0, 8, 2):
            block = np.concatenate(
                [(group == g + e)[:, None] & (band[:, None] == wanted[None, :]) for e in range(2)], axis=1
            )
            spread.append(np.concatenate([block, block], axis=0) * 0.125)
    return high, low, np.stack(spread).astype(BF)


def split(value):
    high = value.astype(BF)
    return high, (value - high.astype(F32)).astype(BF)


def orbitals(coef_ref, cut_x, onehot, pre, pim, tre, tim, mh_ref, ml_ref, e_ref, side, use):
    parts = [coef_ref[:, c, :] for c in range(2)]
    for j in range(2):
        masks = [(cut_x == 8 * j + i).astype(F32).astype(BF) for i in range(8)]
        block = jnp.concatenate([parts[c] * masks[i] for c in range(2) for i in range(8)], axis=0)
        field = lax.dot_general(onehot, block, (((1,), (1,)), ((), ())), preferred_element_type=F32)
        pre[pl.ds(j * PLANE, PLANE), :] = field[:, :LANES]
        pim[pl.ds(j * PLANE, PLANE), :] = field[:, LANES:]

    @pl.loop(0, 4, unroll=4)
    def _(step):
        base = (step // 2) * PLANE + (step % 2) * 8
        at = [pl.ds(pl.multiple_of(base + y * NFFT, 8), 8) for y in range(NFFT)]
        for y, (re, im) in enumerate(fft16([(pre[a, :], pim[a, :]) for a in at], 1)):
            tre[at[y], :] = re
            tim[at[y], :] = im

    @pl.loop(0, 4, unroll=4)
    def _(step):
        base = pl.multiple_of(step * 128, 128)
        got = fft16(
            [(tre[pl.ds(base + z, 8, stride=NFFT), :], tim[pl.ds(base + z, 8, stride=NFFT), :]) for z in range(NFFT)], 1
        )
        for z, (re, im) in enumerate(got):
            pre[pl.ds(base + z * 8, 8), :] = re
            pim[pl.ds(base + z * 8, 8), :] = im

    halves = [jnp.concatenate([pre[pl.ds(j * PLANE, PLANE), :], pim[pl.ds(j * PLANE, PLANE), :]], axis=1) for j in range(2)]
    for k1, field in enumerate((halves[0] + halves[1], halves[0] - halves[1])):
        high, low = split(field)
        mixed = (
            jnp.dot(high, mh_ref[k1], preferred_element_type=F32)
            + jnp.dot(low, mh_ref[k1], preferred_element_type=F32)
            + jnp.dot(high, ml_ref[k1], preferred_element_type=F32)
        )
        both = jnp.concatenate([mixed[:, :LANES], mixed[:, LANES:]], axis=0)
        lines = jnp.concatenate(split(both), axis=1)
        for h in range(4):
            got = jnp.dot(lines, e_ref[4 * side + h], preferred_element_type=F32)
            for e in range(2):
                column = got[:, e * LANES:(e + 1) * LANES]
                use(k1 + 2 * (2 * h + e), column[:PLANE], column[PLANE:])


def compute(width, count, strip, rows, coef_hbm, vec_hbm, idx_hbm, w_hbm, mh_hbm, ml_hbm, e_hbm, out_ref,
            here_ref, there_ref, vec_ref, idx_ref, w_ref, mh_ref, ml_ref, e_ref,
            ore, oim, pre, pim, qre, qim, vgrid, cgrid, vpick, cpick, blocks, slots,
            in_sem, ring_send, ring_recv, send_sem, recv_sem):
    me = lax.axis_index("ga")
    point = lax.axis_index("ka")
    pairs = [(vec_hbm, vec_ref), (coef_hbm, here_ref), (idx_hbm, idx_ref), (mh_hbm, mh_ref), (ml_hbm, ml_ref),
             (e_hbm, e_ref), (w_hbm, w_ref)]
    fetch = [pltpu.make_async_copy(src, dst, in_sem.at[n]) for n, (src, dst) in enumerate(pairs)]
    for copy in fetch:
        copy.start()
    barrier = pltpu.get_barrier_semaphore()
    left_point = lax.rem(point + count - 1, count)
    pl.semaphore_signal(barrier, inc=1, device_id={"ka": left_point}, device_id_type=MESH)
    for step in range(1, width):
        pl.semaphore_signal(barrier, inc=1, device_id={"ga": lax.rem(me + step, width)}, device_id_type=MESH)
    pl.semaphore_wait(barrier, width)
    ring = pltpu.make_async_remote_copy(
        src_ref=coef_hbm,
        dst_ref=there_ref,
        send_sem=ring_send,
        recv_sem=ring_recv,
        device_id={"ka": lax.rem(point + 1, count)},
        device_id_type=MESH,
    )
    ring.start()
    fetch[0].wait()
    fetch[1].wait()
    waves = vec_ref.shape[1]
    index = vec_ref[...]
    cut_x = index // PLANE
    cut_n = index % PLANE
    points = lax.broadcasted_iota(jnp.int32, (PLANE, waves), 0)
    onehot = jnp.where(points == cut_n, 1.0 / 64, 0.0).astype(BF)
    for copy in fetch[2:]:
        copy.wait()

    def keep(x, re, im):
        ore[pl.ds(x * PLANE, PLANE), :] = re
        oim[pl.ds(x * PLANE, PLANE), :] = im

    def multiply(x, re, im):
        at = pl.ds(x * PLANE, PLANE)
        ar, ai = ore[at, :], oim[at, :]
        qre[at, :] = ar * re + ai * im
        qim[at, :] = ar * im - ai * re

    orbitals(here_ref, cut_x, onehot, pre, pim, vgrid, cgrid, mh_ref, ml_ref, e_ref, 0, keep)
    ring.wait()
    orbitals(there_ref, cut_x, onehot, pre, pim, vgrid, cgrid, mh_ref, ml_ref, e_ref, 1, multiply)

    @pl.loop(0, 32, unroll=4)
    def _(step):
        at = [pl.ds(pl.multiple_of(x * PLANE + step * 8, 8), 8) for x in range(NFFT)]
        for x, (re, im) in enumerate(fft16([(qre[a, :], qim[a, :]) for a in at], -1)):
            vgrid[at[x], :] = re
            cgrid[at[x], :] = im

    @pl.loop(0, 32, unroll=4)
    def _(step):
        at = [pl.ds(pl.multiple_of(step * 128 + z * 8, 8), 8) for z in range(NFFT)]
        for z, (re, im) in enumerate(fft16([(vgrid[a, :], cgrid[a, :]) for a in at], -1)):
            qre[at[z], :] = re
            qim[at[z], :] = im

    left_half = lax.broadcasted_iota(jnp.int32, (8, LANES), 1) < PAIRS

    @pl.loop(0, 32, unroll=4)
    def _(step):
        plane = (step // 2) * PLANE
        half = step % 2
        take = [
            pl.ds(plane + (y // 8) * 128 + half * 64 + y % 8, 8, stride=8) for y in range(NFFT)
        ]
        for y, (re, im) in enumerate(fft16([(qre[a, :], qim[a, :]) for a in take], -1)):
            at = pl.ds(pl.multiple_of(plane + y * NFFT + half * 8, 8), 8)
            vgrid[at, :] = jnp.where(left_half, re, pltpu.roll(im, PAIRS, 1))
            cgrid[at, :] = jnp.where(left_half, pltpu.roll(re, PAIRS, 1), im)

    @pl.loop(0, waves // 32)
    def _(step):
        base = pl.multiple_of(step * 32, 32)
        for u in range(32):
            g = base + u
            vpick[pl.ds(g, 1), :] = vgrid[pl.ds(idx_ref[g], 1), :]

    start = me * strip

    @pl.loop(0, strip // 32)
    def _(step):
        base = pl.multiple_of(step * 32, 32)
        for u in range(32):
            g = base + u
            cpick[pl.ds(g, 1), :] = cgrid[pl.ds(idx_ref[start + g], 1), :]

    screened = jnp.dot(w_ref[...], vpick[...].astype(BF), preferred_element_type=F32).astype(BF)
    left = cpick[...].T.astype(BF)
    cross = jnp.dot(left, screened, preferred_element_type=F32)
    top, bottom = cross[:PAIRS], pltpu.roll(cross[PAIRS:], PAIRS, 1)
    lane = lax.broadcasted_iota(jnp.int32, (PAIRS, LANES), 1)
    total = jnp.where(lane < PAIRS, top + bottom, top - bottom)
    for d in range(width):
        blocks[d] = total[d * rows:(d + 1) * rows]
    copies = []
    for step in range(1, width):
        peer = lax.rem(me + step, width)
        copy = pltpu.make_async_remote_copy(
            src_ref=blocks.at[peer],
            dst_ref=slots.at[step - 1],
            send_sem=send_sem.at[step - 1],
            recv_sem=recv_sem.at[step - 1],
            device_id={"ga": peer},
            device_id_type=MESH,
        )
        copy.start()
        copies.append(copy)
    total = blocks[me]
    for step, copy in enumerate(copies):
        copy.wait_recv()
        total = total + slots[step]
    out_ref[...] = total
    for copy in copies:
        copy.wait_send()


def body(band_coefs, screening, grid_index):
    width = lax.axis_size("ga")
    count = lax.axis_size("ka")
    strip, waves = screening.shape[1:]
    rows = PAIRS // width
    here = band_coefs[0]
    high, low, spread = (jnp.asarray(t) for t in tables())
    hbm = pl.BlockSpec(memory_space=pltpu.HBM)
    result = pl.pallas_call(
        functools.partial(compute, width, count, strip, rows),
        out_shape=jax.ShapeDtypeStruct((rows, LANES), F32),
        in_specs=[hbm] * 7,
        out_specs=pl.BlockSpec(memory_space=pltpu.VMEM),
        scratch_shapes=[
            pltpu.VMEM(here.shape, BF),
            pltpu.VMEM(here.shape, BF),
            pltpu.VMEM((1, waves), jnp.int32),
            pltpu.SMEM((waves,), jnp.int32),
            pltpu.VMEM((strip, waves), BF),
            pltpu.VMEM(high.shape, BF),
            pltpu.VMEM(low.shape, BF),
            pltpu.VMEM(spread.shape, BF),
            pltpu.VMEM((GRID, LANES), F32),
            pltpu.VMEM((GRID, LANES), F32),
            pltpu.VMEM((2 * PLANE, LANES), F32),
            pltpu.VMEM((2 * PLANE, LANES), F32),
            pltpu.VMEM((GRID, LANES), F32),
            pltpu.VMEM((GRID, LANES), F32),
            pltpu.VMEM((GRID, LANES), F32),
            pltpu.VMEM((GRID, LANES), F32),
            pltpu.VMEM((waves, LANES), F32),
            pltpu.VMEM((strip, LANES), F32),
            pltpu.VMEM((width, rows, LANES), F32),
            pltpu.VMEM((width - 1, rows, LANES), F32),
            pltpu.SemaphoreType.DMA((7,)),
            pltpu.SemaphoreType.DMA,
            pltpu.SemaphoreType.DMA,
            pltpu.SemaphoreType.DMA((width - 1,)),
            pltpu.SemaphoreType.DMA((width - 1,)),
        ],
        compiler_params=pltpu.CompilerParams(
            collective_id=0, has_side_effects=True, vmem_limit_bytes=56 * 1024 * 1024
        ),
    )(here, grid_index[None], grid_index, screening[0], high, low, spread)
    return (result * (1.0 / math.sqrt(waves)))[None, None]


def solution(mesh):
    return jax.shard_map(
        body,
        mesh=mesh,
        in_specs=(P("ka", None, None, None), P(None, "ga", None), P()),
        out_specs=P("ka", None, "ga", None),
        check_vma=False,
    )
```

```python
import functools
import math

import jax
import jax.numpy as jnp
import numpy as np
from jax import lax
from jax.experimental import pallas as pl
from jax.experimental.pallas import tpu as pltpu
from jax.sharding import PartitionSpec as P

NBND = 8
NFFT = 16
PLANE = NFFT * NFFT
GRID = NFFT * PLANE
PAIRS = NBND * NBND
LANES = 2 * PAIRS
BANDS = 4 * NBND
BF = jnp.bfloat16
F32 = jnp.float32
MESH = pl.DeviceIdType.MESH


def radix4(parts, sign):
    (ar, ai), (br, bi), (cr, ci), (dr, di) = parts
    sr, si = ar + cr, ai + ci
    tr, ti = ar - cr, ai - ci
    ur, ui = br + dr, bi + di
    vr, vi = br - dr, bi - di
    first = (sr + ur, si + ui)
    third = (sr - ur, si - ui)
    plus = (tr - vi, ti + vr)
    minus = (tr + vi, ti - vr)
    if sign > 0:
        return [first, plus, third, minus]
    return [first, minus, third, plus]


def twiddle(value, power, sign):
    re, im = value
    power = (power * (1 if sign > 0 else -1)) % 16
    if power == 0:
        return value
    if power == 4:
        return (-im, re)
    if power == 12:
        return (im, -re)
    cosine = math.cos(2.0 * math.pi * power / 16)
    sine = math.sin(2.0 * math.pi * power / 16)
    if power % 4 == 2:
        half = math.sqrt(0.5)
        p = 1.0 if cosine > 0 else -1.0
        q = 1.0 if sine > 0 else -1.0
        if p == q:
            return ((re - im) * (p * half), (re + im) * (p * half))
        return ((re + im) * (p * half), (im - re) * (p * half))
    return (re * cosine - im * sine, re * sine + im * cosine)


def fft16(values, sign):
    inner = [radix4([values[4 * j + i] for j in range(4)], sign) for i in range(4)]
    out = [None] * 16
    for k1 in range(4):
        parts = [twiddle(inner[i][k1], i * k1, sign) for i in range(4)]
        for k2, got in enumerate(radix4(parts, sign)):
            out[k1 + 4 * k2] = got
    return out


def tables():
    half = BANDS // 2
    group = np.arange(LANES) // half
    band = np.arange(LANES) % half
    same = (band[:, None] == band[None, :]).astype(np.float64)
    mats = []
    for k1 in range(2):
        angle = 2.0 * np.pi * (group[:, None] * (k1 + 2 * group[None, :]) % 16) / 16
        c, s = np.cos(angle) * same, np.sin(angle) * same
        mats.append(np.block([[c, s], [-s, c]]))
    full = np.stack(mats).astype(np.float32)
    high = full.astype(BF)
    low = (full - high.astype(np.float32)).astype(BF)
    lane = np.arange(LANES)
    kind, pair = lane // PAIRS, lane % PAIRS
    spread = []
    for wanted in (kind * NBND + pair // NBND, kind * NBND + pair % NBND):
        for g in range(0, 8, 2):
            block = np.concatenate(
                [(group == g + e)[:, None] & (band[:, None] == wanted[None, :]) for e in range(2)], axis=1
            )
            spread.append(np.concatenate([block, block], axis=0) * 0.125)
    return high, low, np.stack(spread).astype(BF)


def split(value):
    high = value.astype(BF)
    return high, (value - high.astype(F32)).astype(BF)


def orbitals(coef_ref, cut_x, onehot, pre, pim, tre, tim, mh_ref, ml_ref, e_ref, side, use, arrive):
    waves = cut_x.shape[1]
    chunk = waves // len(arrive)
    fields = [None, None]
    for n, ready in enumerate(arrive):
        ready()
        at = slice(n * chunk, (n + 1) * chunk)
        parts = [coef_ref[:, c, at] for c in range(2)]
        for j in range(2):
            masks = [(cut_x[:, at] == 8 * j + i).astype(F32).astype(BF) for i in range(8)]
            block = jnp.concatenate([parts[c] * masks[i] for c in range(2) for i in range(8)], axis=0)
            got = lax.dot_general(onehot[:, at], block, (((1,), (1,)), ((), ())), preferred_element_type=F32)
            fields[j] = got if n == 0 else fields[j] + got
    for j in range(2):
        pre[pl.ds(j * PLANE, PLANE), :] = fields[j][:, :LANES]
        pim[pl.ds(j * PLANE, PLANE), :] = fields[j][:, LANES:]

    @pl.loop(0, 4, unroll=4)
    def _(step):
        base = (step // 2) * PLANE + (step % 2) * 8
        at = [pl.ds(pl.multiple_of(base + y * NFFT, 8), 8) for y in range(NFFT)]
        for y, (re, im) in enumerate(fft16([(pre[a, :], pim[a, :]) for a in at], 1)):
            tre[at[y], :] = re
            tim[at[y], :] = im

    @pl.loop(0, 4, unroll=4)
    def _(step):
        base = pl.multiple_of(step * 128, 128)
        got = fft16(
            [(tre[pl.ds(base + z, 8, stride=NFFT), :], tim[pl.ds(base + z, 8, stride=NFFT), :]) for z in range(NFFT)], 1
        )
        for z, (re, im) in enumerate(got):
            pre[pl.ds(base + z * 8, 8), :] = re
            pim[pl.ds(base + z * 8, 8), :] = im

    halves = [jnp.concatenate([pre[pl.ds(j * PLANE, PLANE), :], pim[pl.ds(j * PLANE, PLANE), :]], axis=1) for j in range(2)]
    for k1, field in enumerate((halves[0] + halves[1], halves[0] - halves[1])):
        high, low = split(field)
        mixed = (
            jnp.dot(high, mh_ref[k1], preferred_element_type=F32)
            + jnp.dot(low, mh_ref[k1], preferred_element_type=F32)
            + jnp.dot(high, ml_ref[k1], preferred_element_type=F32)
        )
        both = jnp.concatenate([mixed[:, :LANES], mixed[:, LANES:]], axis=0)
        lines = jnp.concatenate(split(both), axis=1)
        for h in range(4):
            got = jnp.dot(lines, e_ref[4 * side + h], preferred_element_type=F32)
            for e in range(2):
                column = got[:, e * LANES:(e + 1) * LANES]
                use(k1 + 2 * (2 * h + e), column[:PLANE], column[PLANE:])


def compute(width, count, strip, rows, coef_hbm, vec_hbm, idx_hbm, w_hbm, mh_hbm, ml_hbm, e_hbm, out_ref,
            here_ref, there_ref, vec_ref, idx_ref, w_ref, mh_ref, ml_ref, e_ref,
            ore, oim, pre, pim, qre, qim, vgrid, cgrid, vpick, cpick, blocks, slots,
            in_sem, ring_send, ring_recv, send_sem, recv_sem):
    me = lax.axis_index("ga")
    point = lax.axis_index("ka")
    pairs = [(vec_hbm, vec_ref), (coef_hbm, here_ref), (idx_hbm, idx_ref), (mh_hbm, mh_ref), (ml_hbm, ml_ref),
             (e_hbm, e_ref), (w_hbm, w_ref)]
    fetch = [pltpu.make_async_copy(src, dst, in_sem.at[n]) for n, (src, dst) in enumerate(pairs)]
    barrier = pltpu.get_barrier_semaphore()
    left_point = lax.rem(point + count - 1, count)
    pl.semaphore_signal(barrier, inc=1, device_id={"ka": left_point}, device_id_type=MESH)
    for step in range(1, width):
        pl.semaphore_signal(barrier, inc=1, device_id={"ga": lax.rem(me + step, width)}, device_id_type=MESH)
    for copy in fetch[:2]:
        copy.start()
    pl.semaphore_wait(barrier, width)
    bands, chunk = coef_hbm.shape[0] // 2, coef_hbm.shape[2] // 2
    ring = []
    for n in range(4):
        at = (pl.ds(n % 2 * bands, bands), slice(None), pl.ds(n // 2 * chunk, chunk))
        ring.append(pltpu.make_async_remote_copy(
            src_ref=coef_hbm.at[at],
            dst_ref=there_ref.at[at],
            send_sem=ring_send.at[n],
            recv_sem=ring_recv.at[n],
            device_id={"ka": lax.rem(point + 1, count)},
            device_id_type=MESH,
        ))
        ring[n].start()
    for copy in fetch[2:]:
        copy.start()
    fetch[0].wait()
    fetch[1].wait()
    waves = vec_ref.shape[1]
    index = vec_ref[...]
    cut_x = index // PLANE
    cut_n = index % PLANE
    points = lax.broadcasted_iota(jnp.int32, (PLANE, waves), 0)
    onehot = jnp.where(points == cut_n, 1.0 / 64, 0.0).astype(BF)
    for copy in fetch[2:]:
        copy.wait()

    def keep(x, re, im):
        ore[pl.ds(x * PLANE, PLANE), :] = re
        oim[pl.ds(x * PLANE, PLANE), :] = im

    def multiply(x, re, im):
        at = pl.ds(x * PLANE, PLANE)
        ar, ai = ore[at, :], oim[at, :]
        qre[at, :] = ar * re + ai * im
        qim[at, :] = ar * im - ai * re

    orbitals(here_ref, cut_x, onehot, pre, pim, vgrid, cgrid, mh_ref, ml_ref, e_ref, 0, keep, [lambda: None])
    orbitals(there_ref, cut_x, onehot, pre, pim, vgrid, cgrid, mh_ref, ml_ref, e_ref, 1, multiply,
             [lambda: (ring[0].wait_recv(), ring[1].wait_recv()), lambda: (ring[2].wait_recv(), ring[3].wait_recv())])

    @pl.loop(0, 32, unroll=4)
    def _(step):
        at = [pl.ds(pl.multiple_of(x * PLANE + step * 8, 8), 8) for x in range(NFFT)]
        for x, (re, im) in enumerate(fft16([(qre[a, :], qim[a, :]) for a in at], -1)):
            vgrid[at[x], :] = re
            cgrid[at[x], :] = im

    @pl.loop(0, 32, unroll=4)
    def _(step):
        at = [pl.ds(pl.multiple_of(step * 128 + z * 8, 8), 8) for z in range(NFFT)]
        for z, (re, im) in enumerate(fft16([(vgrid[a, :], cgrid[a, :]) for a in at], -1)):
            qre[at[z], :] = re
            qim[at[z], :] = im

    left_half = lax.broadcasted_iota(jnp.int32, (8, LANES), 1) < PAIRS

    @pl.loop(0, 32, unroll=4)
    def _(step):
        plane = (step // 2) * PLANE
        half = step % 2
        take = [
            pl.ds(plane + (y // 8) * 128 + half * 64 + y % 8, 8, stride=8) for y in range(NFFT)
        ]
        for y, (re, im) in enumerate(fft16([(qre[a, :], qim[a, :]) for a in take], -1)):
            at = pl.ds(pl.multiple_of(plane + y * NFFT + half * 8, 8), 8)
            vgrid[at, :] = jnp.where(left_half, re, pltpu.roll(im, PAIRS, 1))
            cgrid[at, :] = jnp.where(left_half, pltpu.roll(re, PAIRS, 1), im)

    @pl.loop(0, waves // 32)
    def _(step):
        base = pl.multiple_of(step * 32, 32)
        got = [vgrid[pl.ds(idx_ref[base + u], 1), :] for u in range(32)]
        for u in range(32):
            vpick[pl.ds(base + u, 1), :] = got[u]

    start = me * strip

    @pl.loop(0, strip // 32)
    def _(step):
        base = pl.multiple_of(step * 32, 32)
        got = [cgrid[pl.ds(idx_ref[start + base + u], 1), :] for u in range(32)]
        for u in range(32):
            cpick[pl.ds(base + u, 1), :] = got[u]

    screened = jnp.dot(w_ref[...], vpick[...].astype(BF), preferred_element_type=F32).astype(BF)
    left = cpick[...].T.astype(BF)
    cross = jnp.dot(left, screened, preferred_element_type=F32)
    top, bottom = cross[:PAIRS], pltpu.roll(cross[PAIRS:], PAIRS, 1)
    lane = lax.broadcasted_iota(jnp.int32, (PAIRS, LANES), 1)
    total = jnp.where(lane < PAIRS, top + bottom, top - bottom)
    for d in range(width):
        blocks[d] = total[d * rows:(d + 1) * rows]
    copies = []
    for step in range(1, width):
        peer = lax.rem(me + step, width)
        copy = pltpu.make_async_remote_copy(
            src_ref=blocks.at[peer],
            dst_ref=slots.at[step - 1],
            send_sem=send_sem.at[step - 1],
            recv_sem=recv_sem.at[step - 1],
            device_id={"ga": peer},
            device_id_type=MESH,
        )
        copy.start()
        copies.append(copy)
    total = blocks[me]
    for step, copy in enumerate(copies):
        copy.wait_recv()
        total = total + slots[step]
    out_ref[...] = total
    for copy in ring + copies:
        copy.wait_send()


def body(band_coefs, screening, grid_index):
    width = lax.axis_size("ga")
    count = lax.axis_size("ka")
    strip, waves = screening.shape[1:]
    rows = PAIRS // width
    here = band_coefs[0]
    high, low, spread = (jnp.asarray(t) for t in tables())
    hbm = pl.BlockSpec(memory_space=pltpu.HBM)
    result = pl.pallas_call(
        functools.partial(compute, width, count, strip, rows),
        out_shape=jax.ShapeDtypeStruct((rows, LANES), F32),
        in_specs=[hbm] * 7,
        out_specs=pl.BlockSpec(memory_space=pltpu.VMEM),
        scratch_shapes=[
            pltpu.VMEM(here.shape, BF),
            pltpu.VMEM(here.shape, BF),
            pltpu.VMEM((1, waves), jnp.int32),
            pltpu.SMEM((waves,), jnp.int32),
            pltpu.VMEM((strip, waves), BF),
            pltpu.VMEM(high.shape, BF),
            pltpu.VMEM(low.shape, BF),
            pltpu.VMEM(spread.shape, BF),
            pltpu.VMEM((GRID, LANES), F32),
            pltpu.VMEM((GRID, LANES), F32),
            pltpu.VMEM((2 * PLANE, LANES), F32),
            pltpu.VMEM((2 * PLANE, LANES), F32),
            pltpu.VMEM((GRID, LANES), F32),
            pltpu.VMEM((GRID, LANES), F32),
            pltpu.VMEM((GRID, LANES), F32),
            pltpu.VMEM((GRID, LANES), F32),
            pltpu.VMEM((waves, LANES), F32),
            pltpu.VMEM((strip, LANES), F32),
            pltpu.VMEM((width, rows, LANES), F32),
            pltpu.VMEM((width - 1, rows, LANES), F32),
            pltpu.SemaphoreType.DMA((7,)),
            pltpu.SemaphoreType.DMA((4,)),
            pltpu.SemaphoreType.DMA((4,)),
            pltpu.SemaphoreType.DMA((width - 1,)),
            pltpu.SemaphoreType.DMA((width - 1,)),
        ],
        compiler_params=pltpu.CompilerParams(
            collective_id=0, has_side_effects=True, vmem_limit_bytes=56 * 1024 * 1024
        ),
    )(here, grid_index[None], grid_index, screening[0], high, low, spread)
    return (result * (1.0 / math.sqrt(waves)))[None, None]


def solution(mesh):
    return jax.shard_map(
        body,
        mesh=mesh,
        in_specs=(P("ka", None, None, None), P(None, "ga", None), P()),
        out_specs=P("ka", None, "ga", None),
        check_vma=False,
    )
```

```python
import functools
import math

import jax
import jax.numpy as jnp
import numpy as np
from jax import lax
from jax.experimental import pallas as pl
from jax.experimental.pallas import tpu as pltpu
from jax.sharding import PartitionSpec as P

NBND = 8
NFFT = 16
PLANE = NFFT * NFFT
GRID = NFFT * PLANE
PAIRS = NBND * NBND
LANES = 2 * PAIRS
BANDS = 4 * NBND
BF = jnp.bfloat16
F32 = jnp.float32
MESH = pl.DeviceIdType.MESH


def radix4(parts, sign):
    (ar, ai), (br, bi), (cr, ci), (dr, di) = parts
    sr, si = ar + cr, ai + ci
    tr, ti = ar - cr, ai - ci
    ur, ui = br + dr, bi + di
    vr, vi = br - dr, bi - di
    first = (sr + ur, si + ui)
    third = (sr - ur, si - ui)
    plus = (tr - vi, ti + vr)
    minus = (tr + vi, ti - vr)
    if sign > 0:
        return [first, plus, third, minus]
    return [first, minus, third, plus]


def twiddle(value, power, sign):
    re, im = value
    power = (power * (1 if sign > 0 else -1)) % 16
    if power == 0:
        return value
    if power == 4:
        return (-im, re)
    if power == 12:
        return (im, -re)
    cosine = math.cos(2.0 * math.pi * power / 16)
    sine = math.sin(2.0 * math.pi * power / 16)
    if power % 4 == 2:
        half = math.sqrt(0.5)
        p = 1.0 if cosine > 0 else -1.0
        q = 1.0 if sine > 0 else -1.0
        if p == q:
            return ((re - im) * (p * half), (re + im) * (p * half))
        return ((re + im) * (p * half), (im - re) * (p * half))
    return (re * cosine - im * sine, re * sine + im * cosine)


def fft16(values, sign):
    inner = [radix4([values[4 * j + i] for j in range(4)], sign) for i in range(4)]
    out = [None] * 16
    for k1 in range(4):
        parts = [twiddle(inner[i][k1], i * k1, sign) for i in range(4)]
        for k2, got in enumerate(radix4(parts, sign)):
            out[k1 + 4 * k2] = got
    return out


def tables():
    half = BANDS // 2
    group = np.arange(LANES) // half
    band = np.arange(LANES) % half
    same = (band[:, None] == band[None, :]).astype(np.float64)
    mats = []
    for k1 in range(2):
        angle = 2.0 * np.pi * (group[:, None] * (k1 + 2 * group[None, :]) % 16) / 16
        c, s = np.cos(angle) * same, np.sin(angle) * same
        mats.append(np.block([[c, s], [-s, c]]))
    full = np.stack(mats).astype(np.float32)
    high = full.astype(BF)
    low = (full - high.astype(np.float32)).astype(BF)
    lane = np.arange(LANES)
    kind, pair = lane // PAIRS, lane % PAIRS
    spread = []
    for wanted in (kind * NBND + pair // NBND, kind * NBND + pair % NBND):
        for g in range(0, 8, 2):
            block = np.concatenate(
                [(group == g + e)[:, None] & (band[:, None] == wanted[None, :]) for e in range(2)], axis=1
            )
            spread.append(np.concatenate([block, block], axis=0) * 0.125)
    return high, low, np.stack(spread).astype(BF)


def split(value):
    high = value.astype(BF)
    return high, (value - high.astype(F32)).astype(BF)


def orbitals(coef_ref, cut_x, onehot, pre, pim, tre, tim, mh_ref, ml_ref, e_ref, side, use, arrive, settle):
    waves = cut_x.shape[1]
    chunk = waves // len(arrive)
    fields = [None, None]
    for n, ready in enumerate(arrive):
        ready()
        at = slice(n * chunk, (n + 1) * chunk)
        parts = [coef_ref[:, c, at] for c in range(2)]
        for j in range(2):
            masks = [(cut_x[:, at] == 8 * j + i).astype(F32).astype(BF) for i in range(8)]
            block = jnp.concatenate([parts[c] * masks[i] for c in range(2) for i in range(8)], axis=0)
            got = lax.dot_general(onehot[:, at], block, (((1,), (1,)), ((), ())), preferred_element_type=F32)
            fields[j] = got if n == 0 else fields[j] + got
    for j in range(2):
        pre[pl.ds(j * PLANE, PLANE), :] = fields[j][:, :LANES]
        pim[pl.ds(j * PLANE, PLANE), :] = fields[j][:, LANES:]

    @pl.loop(0, 4, unroll=4)
    def _(step):
        base = (step // 2) * PLANE + (step % 2) * 8
        at = [pl.ds(pl.multiple_of(base + y * NFFT, 8), 8) for y in range(NFFT)]
        for y, (re, im) in enumerate(fft16([(pre[a, :], pim[a, :]) for a in at], 1)):
            tre[at[y], :] = re
            tim[at[y], :] = im

    @pl.loop(0, 4, unroll=4)
    def _(step):
        base = pl.multiple_of(step * 128, 128)
        got = fft16(
            [(tre[pl.ds(base + z, 8, stride=NFFT), :], tim[pl.ds(base + z, 8, stride=NFFT), :]) for z in range(NFFT)], 1
        )
        for z, (re, im) in enumerate(got):
            pre[pl.ds(base + z * 8, 8), :] = re
            pim[pl.ds(base + z * 8, 8), :] = im

    settle()
    halves = [jnp.concatenate([pre[pl.ds(j * PLANE, PLANE), :], pim[pl.ds(j * PLANE, PLANE), :]], axis=1) for j in range(2)]
    for k1, field in enumerate((halves[0] + halves[1], halves[0] - halves[1])):
        high, low = split(field)
        mixed = (
            jnp.dot(high, mh_ref[k1], preferred_element_type=F32)
            + jnp.dot(low, mh_ref[k1], preferred_element_type=F32)
            + jnp.dot(high, ml_ref[k1], preferred_element_type=F32)
        )
        both = jnp.concatenate([mixed[:, :LANES], mixed[:, LANES:]], axis=0)
        lines = jnp.concatenate(split(both), axis=1)
        for h in range(4):
            got = jnp.dot(lines, e_ref[4 * side + h], preferred_element_type=F32)
            for e in range(2):
                column = got[:, e * LANES:(e + 1) * LANES]
                use(k1 + 2 * (2 * h + e), column[:PLANE], column[PLANE:])


def compute(width, count, strip, rows, coef_hbm, vec_hbm, idx_hbm, w_hbm, mh_hbm, ml_hbm, e_hbm, out_ref,
            here_ref, there_ref, vec_ref, idx_ref, w_ref, mh_ref, ml_ref, e_ref,
            ore, oim, pre, pim, qre, qim, vgrid, cgrid, vpick, cpick, blocks, slots,
            in_sem, ring_send, ring_recv, send_sem, recv_sem):
    me = lax.axis_index("ga")
    point = lax.axis_index("ka")
    pairs = [(vec_hbm, vec_ref), (coef_hbm, here_ref), (idx_hbm, idx_ref), (mh_hbm, mh_ref), (ml_hbm, ml_ref),
             (e_hbm, e_ref), (w_hbm, w_ref)]
    fetch = [pltpu.make_async_copy(src, dst, in_sem.at[n]) for n, (src, dst) in enumerate(pairs)]
    barrier = pltpu.get_barrier_semaphore()
    left_point = lax.rem(point + count - 1, count)
    pl.semaphore_signal(barrier, inc=1, device_id={"ka": left_point}, device_id_type=MESH)
    for step in range(1, width):
        pl.semaphore_signal(barrier, inc=1, device_id={"ga": lax.rem(me + step, width)}, device_id_type=MESH)
    for copy in fetch:
        copy.start()
    pl.semaphore_wait(barrier, width)
    bands, chunk = coef_hbm.shape[0] // 2, coef_hbm.shape[2] // 2
    ring = []
    for n in range(4):
        at = (pl.ds(n % 2 * bands, bands), slice(None), pl.ds(n // 2 * chunk, chunk))
        ring.append(pltpu.make_async_remote_copy(
            src_ref=coef_hbm.at[at],
            dst_ref=there_ref.at[at],
            send_sem=ring_send.at[n],
            recv_sem=ring_recv.at[n],
            device_id={"ka": lax.rem(point + 1, count)},
            device_id_type=MESH,
        ))
        ring[n].start()
    fetch[0].wait()
    fetch[1].wait()
    waves = vec_ref.shape[1]
    index = vec_ref[...]
    cut_x = index // PLANE
    cut_n = index % PLANE
    points = lax.broadcasted_iota(jnp.int32, (PLANE, waves), 0)
    onehot = jnp.where(points == cut_n, 1.0 / 64, 0.0).astype(BF)
    def keep(x, re, im):
        ore[pl.ds(x * PLANE, PLANE), :] = re
        oim[pl.ds(x * PLANE, PLANE), :] = im

    def multiply(x, re, im):
        at = pl.ds(x * PLANE, PLANE)
        ar, ai = ore[at, :], oim[at, :]
        qre[at, :] = ar * re + ai * im
        qim[at, :] = ar * im - ai * re

    orbitals(here_ref, cut_x, onehot, pre, pim, vgrid, cgrid, mh_ref, ml_ref, e_ref, 0, keep, [lambda: None],
             lambda: [copy.wait() for copy in fetch[3:6]])
    orbitals(there_ref, cut_x, onehot, pre, pim, vgrid, cgrid, mh_ref, ml_ref, e_ref, 1, multiply,
             [lambda: (ring[0].wait_recv(), ring[1].wait_recv()), lambda: (ring[2].wait_recv(), ring[3].wait_recv())], lambda: None)

    @pl.loop(0, 32, unroll=4)
    def _(step):
        at = [pl.ds(pl.multiple_of(x * PLANE + step * 8, 8), 8) for x in range(NFFT)]
        for x, (re, im) in enumerate(fft16([(qre[a, :], qim[a, :]) for a in at], -1)):
            vgrid[at[x], :] = re
            cgrid[at[x], :] = im

    @pl.loop(0, 32, unroll=4)
    def _(step):
        at = [pl.ds(pl.multiple_of(step * 128 + z * 8, 8), 8) for z in range(NFFT)]
        for z, (re, im) in enumerate(fft16([(vgrid[a, :], cgrid[a, :]) for a in at], -1)):
            qre[at[z], :] = re
            qim[at[z], :] = im

    left_half = lax.broadcasted_iota(jnp.int32, (8, LANES), 1) < PAIRS

    @pl.loop(0, 32, unroll=4)
    def _(step):
        plane = (step // 2) * PLANE
        half = step % 2
        take = [
            pl.ds(plane + (y // 8) * 128 + half * 64 + y % 8, 8, stride=8) for y in range(NFFT)
        ]
        for y, (re, im) in enumerate(fft16([(qre[a, :], qim[a, :]) for a in take], -1)):
            at = pl.ds(pl.multiple_of(plane + y * NFFT + half * 8, 8), 8)
            vgrid[at, :] = jnp.where(left_half, re, pltpu.roll(im, PAIRS, 1))
            cgrid[at, :] = jnp.where(left_half, pltpu.roll(re, PAIRS, 1), im)

    fetch[2].wait()

    @pl.loop(0, waves // 32)
    def _(step):
        base = pl.multiple_of(step * 32, 32)
        got = [vgrid[pl.ds(idx_ref[base + u], 1), :] for u in range(32)]
        for u in range(32):
            vpick[pl.ds(base + u, 1), :] = got[u]

    start = me * strip

    @pl.loop(0, strip // 32)
    def _(step):
        base = pl.multiple_of(step * 32, 32)
        got = [cgrid[pl.ds(idx_ref[start + base + u], 1), :] for u in range(32)]
        for u in range(32):
            cpick[pl.ds(base + u, 1), :] = got[u]

    fetch[6].wait()
    screened = jnp.dot(w_ref[...], vpick[...].astype(BF), preferred_element_type=F32).astype(BF)
    left = cpick[...].T.astype(BF)
    cross = jnp.dot(left, screened, preferred_element_type=F32)
    top, bottom = cross[:PAIRS], pltpu.roll(cross[PAIRS:], PAIRS, 1)
    lane = lax.broadcasted_iota(jnp.int32, (PAIRS, LANES), 1)
    total = jnp.where(lane < PAIRS, top + bottom, top - bottom)
    for d in range(width):
        blocks[d] = total[d * rows:(d + 1) * rows]
    copies = []
    for step in range(1, width):
        peer = lax.rem(me + step, width)
        copy = pltpu.make_async_remote_copy(
            src_ref=blocks.at[peer],
            dst_ref=slots.at[step - 1],
            send_sem=send_sem.at[step - 1],
            recv_sem=recv_sem.at[step - 1],
            device_id={"ga": peer},
            device_id_type=MESH,
        )
        copy.start()
        copies.append(copy)
    total = blocks[me]
    for step, copy in enumerate(copies):
        copy.wait_recv()
        total = total + slots[step]
    out_ref[...] = total
    for copy in ring + copies:
        copy.wait_send()


def body(band_coefs, screening, grid_index):
    width = lax.axis_size("ga")
    count = lax.axis_size("ka")
    strip, waves = screening.shape[1:]
    rows = PAIRS // width
    here = band_coefs[0]
    high, low, spread = (jnp.asarray(t) for t in tables())
    hbm = pl.BlockSpec(memory_space=pltpu.HBM)
    result = pl.pallas_call(
        functools.partial(compute, width, count, strip, rows),
        out_shape=jax.ShapeDtypeStruct((rows, LANES), F32),
        in_specs=[hbm] * 7,
        out_specs=pl.BlockSpec(memory_space=pltpu.VMEM),
        scratch_shapes=[
            pltpu.VMEM(here.shape, BF),
            pltpu.VMEM(here.shape, BF),
            pltpu.VMEM((1, waves), jnp.int32),
            pltpu.SMEM((waves,), jnp.int32),
            pltpu.VMEM((strip, waves), BF),
            pltpu.VMEM(high.shape, BF),
            pltpu.VMEM(low.shape, BF),
            pltpu.VMEM(spread.shape, BF),
            pltpu.VMEM((GRID, LANES), F32),
            pltpu.VMEM((GRID, LANES), F32),
            pltpu.VMEM((2 * PLANE, LANES), F32),
            pltpu.VMEM((2 * PLANE, LANES), F32),
            pltpu.VMEM((GRID, LANES), F32),
            pltpu.VMEM((GRID, LANES), F32),
            pltpu.VMEM((GRID, LANES), F32),
            pltpu.VMEM((GRID, LANES), F32),
            pltpu.VMEM((waves, LANES), F32),
            pltpu.VMEM((strip, LANES), F32),
            pltpu.VMEM((width, rows, LANES), F32),
            pltpu.VMEM((width - 1, rows, LANES), F32),
            pltpu.SemaphoreType.DMA((7,)),
            pltpu.SemaphoreType.DMA((4,)),
            pltpu.SemaphoreType.DMA((4,)),
            pltpu.SemaphoreType.DMA((width - 1,)),
            pltpu.SemaphoreType.DMA((width - 1,)),
        ],
        compiler_params=pltpu.CompilerParams(
            collective_id=0, has_side_effects=True, vmem_limit_bytes=56 * 1024 * 1024
        ),
    )(here, grid_index[None], grid_index, screening[0], high, low, spread)
    return (result * (1.0 / math.sqrt(waves)))[None, None]


def solution(mesh):
    return jax.shard_map(
        body,
        mesh=mesh,
        in_specs=(P("ka", None, None, None), P(None, "ga", None), P()),
        out_specs=P("ka", None, "ga", None),
        check_vma=False,
    )
```

```python
import functools
import math

import jax
import jax.numpy as jnp
import numpy as np
from jax import lax
from jax.experimental import pallas as pl
from jax.experimental.pallas import tpu as pltpu
from jax.sharding import PartitionSpec as P

NBND = 8
NFFT = 16
PLANE = NFFT * NFFT
GRID = NFFT * PLANE
PAIRS = NBND * NBND
LANES = 2 * PAIRS
BANDS = 4 * NBND
SKEW = 9
BF = jnp.bfloat16
F32 = jnp.float32
MESH = pl.DeviceIdType.MESH


def radix4(parts, sign):
    (ar, ai), (br, bi), (cr, ci), (dr, di) = parts
    sr, si = ar + cr, ai + ci
    tr, ti = ar - cr, ai - ci
    ur, ui = br + dr, bi + di
    vr, vi = br - dr, bi - di
    first = (sr + ur, si + ui)
    third = (sr - ur, si - ui)
    plus = (tr - vi, ti + vr)
    minus = (tr + vi, ti - vr)
    if sign > 0:
        return [first, plus, third, minus]
    return [first, minus, third, plus]


def twiddle(value, power, sign):
    re, im = value
    power = (power * (1 if sign > 0 else -1)) % 16
    if power == 0:
        return value
    if power == 4:
        return (-im, re)
    if power == 12:
        return (im, -re)
    cosine = math.cos(2.0 * math.pi * power / 16)
    sine = math.sin(2.0 * math.pi * power / 16)
    if power % 4 == 2:
        half = math.sqrt(0.5)
        p = 1.0 if cosine > 0 else -1.0
        q = 1.0 if sine > 0 else -1.0
        if p == q:
            return ((re - im) * (p * half), (re + im) * (p * half))
        return ((re + im) * (p * half), (im - re) * (p * half))
    return (re * cosine - im * sine, re * sine + im * cosine)


def fft16(values, sign):
    inner = [radix4([values[4 * j + i] for j in range(4)], sign) for i in range(4)]
    out = [None] * 16
    for k1 in range(4):
        parts = [twiddle(inner[i][k1], i * k1, sign) for i in range(4)]
        for k2, got in enumerate(radix4(parts, sign)):
            out[k1 + 4 * k2] = got
    return out


def tables():
    half = BANDS // 2
    group = np.arange(LANES) // half
    band = np.arange(LANES) % half
    same = (band[:, None] == band[None, :]).astype(np.float64)
    mats = []
    for k1 in range(2):
        angle = 2.0 * np.pi * (group[:, None] * (k1 + 2 * group[None, :]) % 16) / 16
        c, s = np.cos(angle) * same, np.sin(angle) * same
        mats.append(np.block([[c, s], [-s, c]]))
    full = np.stack(mats).astype(np.float32)
    high = full.astype(BF)
    low = (full - high.astype(np.float32)).astype(BF)
    lane = np.arange(LANES)
    kind, pair = lane // PAIRS, lane % PAIRS
    spread = []
    for wanted in (kind * NBND + pair // NBND, kind * NBND + pair % NBND):
        for g in range(0, 8, 2):
            block = np.concatenate(
                [(group == g + e)[:, None] & (band[:, None] == wanted[None, :]) for e in range(2)], axis=1
            )
            spread.append(np.concatenate([block, block], axis=0) * 0.125)
    return high, low, np.stack(spread).astype(BF)


def split(value):
    high = value.astype(BF)
    return high, (value - high.astype(F32)).astype(BF)


def orbitals(coef_ref, cut_x, onehot, pre, pim, tre, tim, mh_ref, ml_ref, e_ref, side, use, arrive, settle):
    waves = cut_x.shape[1]
    chunk = waves // len(arrive)
    fields = [None, None]
    for n, ready in enumerate(arrive):
        ready()
        at = slice(n * chunk, (n + 1) * chunk)
        parts = [coef_ref[:, c, at] for c in range(2)]
        for j in range(2):
            masks = [(cut_x[:, at] == 8 * j + i).astype(F32).astype(BF) for i in range(8)]
            block = jnp.concatenate([parts[c] * masks[i] for c in range(2) for i in range(8)], axis=0)
            got = lax.dot_general(onehot[:, at], block, (((1,), (1,)), ((), ())), preferred_element_type=F32)
            fields[j] = got if n == 0 else fields[j] + got
    for j in range(2):
        pre[pl.ds(j * PLANE, PLANE), :] = fields[j][:, :LANES]
        pim[pl.ds(j * PLANE, PLANE), :] = fields[j][:, LANES:]

    @pl.loop(0, 4, unroll=4)
    def _(step):
        base = (step // 2) * PLANE + (step % 2) * 8
        at = [pl.ds(pl.multiple_of(base + y * NFFT, 8), 8) for y in range(NFFT)]
        for y, (re, im) in enumerate(fft16([(pre[a, :], pim[a, :]) for a in at], 1)):
            tre[at[y], :] = re
            tim[at[y], :] = im

    @pl.loop(0, 4, unroll=4)
    def _(step):
        base = pl.multiple_of(step * 128, 128)
        got = fft16(
            [(tre[pl.ds(base + z, 8, stride=NFFT), :], tim[pl.ds(base + z, 8, stride=NFFT), :]) for z in range(NFFT)], 1
        )
        for z, (re, im) in enumerate(got):
            pre[pl.ds(base + z * 8, 8), :] = re
            pim[pl.ds(base + z * 8, 8), :] = im

    settle()
    halves = [jnp.concatenate([pre[pl.ds(j * PLANE, PLANE), :], pim[pl.ds(j * PLANE, PLANE), :]], axis=1) for j in range(2)]
    for k1, field in enumerate((halves[0] + halves[1], halves[0] - halves[1])):
        high, low = split(field)
        mixed = (
            jnp.dot(high, mh_ref[k1], preferred_element_type=F32)
            + jnp.dot(low, mh_ref[k1], preferred_element_type=F32)
            + jnp.dot(high, ml_ref[k1], preferred_element_type=F32)
        )
        both = jnp.concatenate([mixed[:, :LANES], mixed[:, LANES:]], axis=0)
        lines = jnp.concatenate(split(both), axis=1)
        for h in range(4):
            got = jnp.dot(lines, e_ref[4 * side + h], preferred_element_type=F32)
            for e in range(2):
                column = got[:, e * LANES:(e + 1) * LANES]
                use(k1 + 2 * (2 * h + e), column[:PLANE], column[PLANE:])


def compute(width, count, strip, rows, coef_hbm, vec_hbm, idx_hbm, w_hbm, mh_hbm, ml_hbm, e_hbm, out_ref,
            here_ref, there_ref, vec_ref, idx_ref, w_ref, mh_ref, ml_ref, e_ref,
            ore, oim, pre, pim, qre, qim, vgrid, cgrid, vpick, cpick, blocks, slots,
            in_sem, ring_send, ring_recv, send_sem, recv_sem):
    me = lax.axis_index("ga")
    point = lax.axis_index("ka")
    pairs = [(vec_hbm, vec_ref), (coef_hbm, here_ref), (idx_hbm, idx_ref), (mh_hbm, mh_ref), (ml_hbm, ml_ref),
             (e_hbm, e_ref), (w_hbm, w_ref)]
    fetch = [pltpu.make_async_copy(src, dst, in_sem.at[n]) for n, (src, dst) in enumerate(pairs)]
    barrier = pltpu.get_barrier_semaphore()
    left_point = lax.rem(point + count - 1, count)
    pl.semaphore_signal(barrier, inc=1, device_id={"ka": left_point}, device_id_type=MESH)
    for step in range(1, width):
        pl.semaphore_signal(barrier, inc=1, device_id={"ga": lax.rem(me + step, width)}, device_id_type=MESH)
    for copy in fetch:
        copy.start()
    pl.semaphore_wait(barrier, width)
    bands, chunk = coef_hbm.shape[0] // 2, coef_hbm.shape[2] // 2
    ring = []
    for n in range(4):
        at = (pl.ds(n % 2 * bands, bands), slice(None), pl.ds(n // 2 * chunk, chunk))
        ring.append(pltpu.make_async_remote_copy(
            src_ref=coef_hbm.at[at],
            dst_ref=there_ref.at[at],
            send_sem=ring_send.at[n],
            recv_sem=ring_recv.at[n],
            device_id={"ka": lax.rem(point + 1, count)},
            device_id_type=MESH,
        ))
        ring[n].start()
    fetch[0].wait()
    fetch[1].wait()
    waves = vec_ref.shape[1]
    index = vec_ref[...]
    cut_x = index // PLANE
    cut_n = index % PLANE
    points = lax.broadcasted_iota(jnp.int32, (PLANE, waves), 0)
    onehot = jnp.where(points == cut_n, 1.0 / 64, 0.0).astype(BF)
    def keep(x, re, im):
        ore[pl.ds(x * PLANE, PLANE), :] = re
        oim[pl.ds(x * PLANE, PLANE), :] = im

    def multiply(x, re, im):
        at = pl.ds(x * PLANE, PLANE)
        ar, ai = ore[at, :], oim[at, :]
        qre[at, :] = ar * re + ai * im
        qim[at, :] = ar * im - ai * re

    orbitals(here_ref, cut_x, onehot, pre, pim, vgrid, cgrid, mh_ref, ml_ref, e_ref, 0, keep, [lambda: None],
             lambda: [copy.wait() for copy in fetch[3:6]])
    orbitals(there_ref, cut_x, onehot, pre, pim, vgrid, cgrid, mh_ref, ml_ref, e_ref, 1, multiply,
             [lambda: (ring[0].wait_recv(), ring[1].wait_recv()), lambda: (ring[2].wait_recv(), ring[3].wait_recv())], lambda: None)

    @pl.loop(0, 32, unroll=4)
    def _(step):
        at = [pl.ds(pl.multiple_of(x * PLANE + step * 8, 8), 8) for x in range(NFFT)]
        for x, (re, im) in enumerate(fft16([(qre[a, :], qim[a, :]) for a in at], -1)):
            vgrid[at[x], :] = re
            cgrid[at[x], :] = im

    @pl.loop(0, 32, unroll=4)
    def _(step):
        at = [pl.ds(pl.multiple_of(step * 128 + z * 8, 8), 8) for z in range(NFFT)]
        for z, (re, im) in enumerate(fft16([(vgrid[a, :], cgrid[a, :]) for a in at], -1)):
            to = pl.ds(step * 16 * SKEW + z * SKEW, 8)
            qre[to, :] = re
            qim[to, :] = im

    left_half = lax.broadcasted_iota(jnp.int32, (8, LANES), 1) < PAIRS

    @pl.loop(0, 32, unroll=4)
    def _(step):
        plane = (step // 2) * PLANE
        skewed = (step // 2) * 32 * SKEW
        half = step % 2
        take = [
            pl.ds(skewed + (y // 8) * 16 * SKEW + half * 8 * SKEW + y % 8, 8, stride=SKEW) for y in range(NFFT)
        ]
        for y, (re, im) in enumerate(fft16([(qre[a, :], qim[a, :]) for a in take], -1)):
            at = pl.ds(pl.multiple_of(plane + y * NFFT + half * 8, 8), 8)
            vgrid[at, :] = jnp.where(left_half, re, pltpu.roll(im, PAIRS, 1))
            cgrid[at, :] = jnp.where(left_half, pltpu.roll(re, PAIRS, 1), im)

    fetch[2].wait()

    @pl.loop(0, waves // 32)
    def _(step):
        base = pl.multiple_of(step * 32, 32)
        got = [vgrid[pl.ds(idx_ref[base + u], 1), :] for u in range(32)]
        for u in range(32):
            vpick[pl.ds(base + u, 1), :] = got[u]

    start = me * strip

    @pl.loop(0, strip // 32)
    def _(step):
        base = pl.multiple_of(step * 32, 32)
        got = [cgrid[pl.ds(idx_ref[start + base + u], 1), :] for u in range(32)]
        for u in range(32):
            cpick[pl.ds(base + u, 1), :] = got[u]

    fetch[6].wait()
    screened = jnp.dot(w_ref[...], vpick[...].astype(BF), preferred_element_type=F32).astype(BF)
    left = cpick[...].T.astype(BF)
    cross = jnp.dot(left, screened, preferred_element_type=F32)
    top, bottom = cross[:PAIRS], pltpu.roll(cross[PAIRS:], PAIRS, 1)
    lane = lax.broadcasted_iota(jnp.int32, (PAIRS, LANES), 1)
    total = jnp.where(lane < PAIRS, top + bottom, top - bottom)
    for d in range(width):
        blocks[d] = total[d * rows:(d + 1) * rows]
    copies = []
    for step in range(1, width):
        peer = lax.rem(me + step, width)
        copy = pltpu.make_async_remote_copy(
            src_ref=blocks.at[peer],
            dst_ref=slots.at[step - 1],
            send_sem=send_sem.at[step - 1],
            recv_sem=recv_sem.at[step - 1],
            device_id={"ga": peer},
            device_id_type=MESH,
        )
        copy.start()
        copies.append(copy)
    total = blocks[me]
    for step, copy in enumerate(copies):
        copy.wait_recv()
        total = total + slots[step]
    out_ref[...] = total
    for copy in ring + copies:
        copy.wait_send()


def body(band_coefs, screening, grid_index):
    width = lax.axis_size("ga")
    count = lax.axis_size("ka")
    strip, waves = screening.shape[1:]
    rows = PAIRS // width
    here = band_coefs[0]
    high, low, spread = (jnp.asarray(t) for t in tables())
    hbm = pl.BlockSpec(memory_space=pltpu.HBM)
    result = pl.pallas_call(
        functools.partial(compute, width, count, strip, rows),
        out_shape=jax.ShapeDtypeStruct((rows, LANES), F32),
        in_specs=[hbm] * 7,
        out_specs=pl.BlockSpec(memory_space=pltpu.VMEM),
        scratch_shapes=[
            pltpu.VMEM(here.shape, BF),
            pltpu.VMEM(here.shape, BF),
            pltpu.VMEM((1, waves), jnp.int32),
            pltpu.SMEM((waves,), jnp.int32),
            pltpu.VMEM((strip, waves), BF),
            pltpu.VMEM(high.shape, BF),
            pltpu.VMEM(low.shape, BF),
            pltpu.VMEM(spread.shape, BF),
            pltpu.VMEM((GRID, LANES), F32),
            pltpu.VMEM((GRID, LANES), F32),
            pltpu.VMEM((2 * PLANE, LANES), F32),
            pltpu.VMEM((2 * PLANE, LANES), F32),
            pltpu.VMEM((32 * 16 * SKEW, LANES), F32),
            pltpu.VMEM((32 * 16 * SKEW, LANES), F32),
            pltpu.VMEM((GRID, LANES), F32),
            pltpu.VMEM((GRID, LANES), F32),
            pltpu.VMEM((waves, LANES), F32),
            pltpu.VMEM((strip, LANES), F32),
            pltpu.VMEM((width, rows, LANES), F32),
            pltpu.VMEM((width - 1, rows, LANES), F32),
            pltpu.SemaphoreType.DMA((7,)),
            pltpu.SemaphoreType.DMA((4,)),
            pltpu.SemaphoreType.DMA((4,)),
            pltpu.SemaphoreType.DMA((width - 1,)),
            pltpu.SemaphoreType.DMA((width - 1,)),
        ],
        compiler_params=pltpu.CompilerParams(
            collective_id=0, has_side_effects=True, vmem_limit_bytes=56 * 1024 * 1024
        ),
    )(here, grid_index[None], grid_index, screening[0], high, low, spread)
    return (result * (1.0 / math.sqrt(waves)))[None, None]


def solution(mesh):
    return jax.shard_map(
        body,
        mesh=mesh,
        in_specs=(P("ka", None, None, None), P(None, "ga", None), P()),
        out_specs=P("ka", None, "ga", None),
        check_vma=False,
    )
```

```python
import functools
import math

import jax
import jax.numpy as jnp
import numpy as np
from jax import lax
from jax.experimental import pallas as pl
from jax.experimental.pallas import tpu as pltpu
from jax.sharding import PartitionSpec as P

NBND = 8
NFFT = 16
PLANE = NFFT * NFFT
GRID = NFFT * PLANE
PAIRS = NBND * NBND
LANES = 2 * PAIRS
BANDS = 4 * NBND
SKEW = 9
BF = jnp.bfloat16
F32 = jnp.float32
MESH = pl.DeviceIdType.MESH


def radix4(parts, sign):
    (ar, ai), (br, bi), (cr, ci), (dr, di) = parts
    sr, si = ar + cr, ai + ci
    tr, ti = ar - cr, ai - ci
    ur, ui = br + dr, bi + di
    vr, vi = br - dr, bi - di
    first = (sr + ur, si + ui)
    third = (sr - ur, si - ui)
    plus = (tr - vi, ti + vr)
    minus = (tr + vi, ti - vr)
    if sign > 0:
        return [first, plus, third, minus]
    return [first, minus, third, plus]


def twiddle(value, power, sign):
    re, im = value
    power = (power * (1 if sign > 0 else -1)) % 16
    if power == 0:
        return value
    if power == 4:
        return (-im, re)
    if power == 12:
        return (im, -re)
    cosine = math.cos(2.0 * math.pi * power / 16)
    sine = math.sin(2.0 * math.pi * power / 16)
    if power % 4 == 2:
        half = math.sqrt(0.5)
        p = 1.0 if cosine > 0 else -1.0
        q = 1.0 if sine > 0 else -1.0
        if p == q:
            return ((re - im) * (p * half), (re + im) * (p * half))
        return ((re + im) * (p * half), (im - re) * (p * half))
    return (re * cosine - im * sine, re * sine + im * cosine)


def fft16(values, sign):
    inner = [radix4([values[4 * j + i] for j in range(4)], sign) for i in range(4)]
    out = [None] * 16
    for k1 in range(4):
        parts = [twiddle(inner[i][k1], i * k1, sign) for i in range(4)]
        for k2, got in enumerate(radix4(parts, sign)):
            out[k1 + 4 * k2] = got
    return out


def tables():
    half = BANDS // 2
    group = np.arange(LANES) // half
    band = np.arange(LANES) % half
    same = (band[:, None] == band[None, :]).astype(np.float64)
    mats = []
    for k1 in range(2):
        angle = 2.0 * np.pi * (group[:, None] * (k1 + 2 * group[None, :]) % 16) / 16
        c, s = np.cos(angle) * same, np.sin(angle) * same
        mats.append(np.block([[c, s], [-s, c]]))
    full = np.stack(mats).astype(np.float32)
    high = full.astype(BF)
    low = (full - high.astype(np.float32)).astype(BF)
    lane = np.arange(LANES)
    kind, pair = lane // PAIRS, lane % PAIRS
    spread = []
    for wanted in (kind * NBND + pair // NBND, kind * NBND + pair % NBND):
        for g in range(0, 8, 2):
            block = np.concatenate(
                [(group == g + e)[:, None] & (band[:, None] == wanted[None, :]) for e in range(2)], axis=1
            )
            spread.append(np.concatenate([block, block], axis=0) * 0.125)
    return high, low, np.stack(spread).astype(BF)


def split(value):
    high = value.astype(BF)
    return high, (value - high.astype(F32)).astype(BF)


def orbitals(coef_ref, cut_x, onehot, pre, pim, tre, tim, mh_ref, ml_ref, e_ref, side, use, arrive, settle):
    waves = cut_x.shape[1]
    chunk = waves // len(arrive)
    fields = [None, None]
    for n, ready in enumerate(arrive):
        ready()
        at = slice(n * chunk, (n + 1) * chunk)
        parts = [coef_ref[:, c, at] for c in range(2)]
        for j in range(2):
            masks = [(cut_x[:, at] == 8 * j + i).astype(F32).astype(BF) for i in range(8)]
            block = jnp.concatenate([parts[c] * masks[i] for c in range(2) for i in range(8)], axis=0)
            got = lax.dot_general(onehot[:, at], block, (((1,), (1,)), ((), ())), preferred_element_type=F32)
            fields[j] = got if n == 0 else fields[j] + got
    for j in range(2):
        pre[pl.ds(j * PLANE, PLANE), :] = fields[j][:, :LANES]
        pim[pl.ds(j * PLANE, PLANE), :] = fields[j][:, LANES:]

    @pl.loop(0, 4, unroll=4)
    def _(step):
        base = (step // 2) * PLANE + (step % 2) * 8
        at = [pl.ds(pl.multiple_of(base + y * NFFT, 8), 8) for y in range(NFFT)]
        for y, (re, im) in enumerate(fft16([(pre[a, :], pim[a, :]) for a in at], 1)):
            tre[at[y], :] = re
            tim[at[y], :] = im

    @pl.loop(0, 4, unroll=4)
    def _(step):
        base = pl.multiple_of(step * 128, 128)
        got = fft16(
            [(tre[pl.ds(base + z, 8, stride=NFFT), :], tim[pl.ds(base + z, 8, stride=NFFT), :]) for z in range(NFFT)], 1
        )
        for z, (re, im) in enumerate(got):
            pre[pl.ds(base + z * 8, 8), :] = re
            pim[pl.ds(base + z * 8, 8), :] = im

    settle()
    halves = [jnp.concatenate([pre[pl.ds(j * PLANE, PLANE), :], pim[pl.ds(j * PLANE, PLANE), :]], axis=1) for j in range(2)]
    for k1, field in enumerate((halves[0] + halves[1], halves[0] - halves[1])):
        high, low = split(field)
        mixed = (
            jnp.dot(high, mh_ref[k1], preferred_element_type=F32)
            + jnp.dot(low, mh_ref[k1], preferred_element_type=F32)
            + jnp.dot(high, ml_ref[k1], preferred_element_type=F32)
        )
        both = jnp.concatenate([mixed[:, :LANES], mixed[:, LANES:]], axis=0)
        lines = jnp.concatenate(split(both), axis=1)
        for h in range(4):
            got = jnp.dot(lines, e_ref[4 * side + h], preferred_element_type=F32)
            for e in range(2):
                column = got[:, e * LANES:(e + 1) * LANES]
                use(k1 + 2 * (2 * h + e), column[:PLANE], column[PLANE:])


def compute(width, count, strip, rows, coef_hbm, vec_hbm, idx_hbm, w_hbm, mh_hbm, ml_hbm, e_hbm, out_ref,
            here_ref, there_ref, vec_ref, idx_ref, w_ref, mh_ref, ml_ref, e_ref,
            ore, oim, pre, pim, qre, qim, vgrid, cgrid, vpick, cpick, mixed, blocks, slots,
            in_sem, ring_send, ring_recv, send_sem, recv_sem):
    me = lax.axis_index("ga")
    point = lax.axis_index("ka")
    pairs = [(vec_hbm, vec_ref), (coef_hbm, here_ref), (idx_hbm, idx_ref), (mh_hbm, mh_ref), (ml_hbm, ml_ref),
             (e_hbm, e_ref), (w_hbm, w_ref)]
    fetch = [pltpu.make_async_copy(src, dst, in_sem.at[n]) for n, (src, dst) in enumerate(pairs)]
    barrier = pltpu.get_barrier_semaphore()
    left_point = lax.rem(point + count - 1, count)
    pl.semaphore_signal(barrier, inc=1, device_id={"ka": left_point}, device_id_type=MESH)
    for step in range(1, width):
        pl.semaphore_signal(barrier, inc=1, device_id={"ga": lax.rem(me + step, width)}, device_id_type=MESH)
    for copy in fetch:
        copy.start()
    pl.semaphore_wait(barrier, width)
    bands, chunk = coef_hbm.shape[0] // 2, coef_hbm.shape[2] // 2
    ring = []
    for n in range(4):
        at = (pl.ds(n % 2 * bands, bands), slice(None), pl.ds(n // 2 * chunk, chunk))
        ring.append(pltpu.make_async_remote_copy(
            src_ref=coef_hbm.at[at],
            dst_ref=there_ref.at[at],
            send_sem=ring_send.at[n],
            recv_sem=ring_recv.at[n],
            device_id={"ka": lax.rem(point + 1, count)},
            device_id_type=MESH,
        ))
        ring[n].start()
    fetch[0].wait()
    fetch[1].wait()
    waves = vec_ref.shape[1]
    index = vec_ref[...]
    cut_x = index // PLANE
    cut_n = index % PLANE
    points = lax.broadcasted_iota(jnp.int32, (PLANE, waves), 0)
    onehot = jnp.where(points == cut_n, 1.0 / 64, 0.0).astype(BF)
    def keep(x, re, im):
        ore[pl.ds(x * PLANE, PLANE), :] = re
        oim[pl.ds(x * PLANE, PLANE), :] = im

    def multiply(x, re, im):
        at = pl.ds(x * PLANE, PLANE)
        ar, ai = ore[at, :], oim[at, :]
        qre[at, :] = ar * re + ai * im
        qim[at, :] = ar * im - ai * re

    orbitals(here_ref, cut_x, onehot, pre, pim, vgrid, cgrid, mh_ref, ml_ref, e_ref, 0, keep, [lambda: None],
             lambda: [copy.wait() for copy in fetch[3:6]])
    orbitals(there_ref, cut_x, onehot, pre, pim, vgrid, cgrid, mh_ref, ml_ref, e_ref, 1, multiply,
             [lambda: (ring[0].wait_recv(), ring[1].wait_recv()), lambda: (ring[2].wait_recv(), ring[3].wait_recv())], lambda: None)

    @pl.loop(0, 32, unroll=4)
    def _(step):
        at = [pl.ds(pl.multiple_of(x * PLANE + step * 8, 8), 8) for x in range(NFFT)]
        for x, (re, im) in enumerate(fft16([(qre[a, :], qim[a, :]) for a in at], -1)):
            vgrid[at[x], :] = re
            cgrid[at[x], :] = im

    @pl.loop(0, 32, unroll=4)
    def _(step):
        at = [pl.ds(pl.multiple_of(step * 128 + z * 8, 8), 8) for z in range(NFFT)]
        for z, (re, im) in enumerate(fft16([(vgrid[a, :], cgrid[a, :]) for a in at], -1)):
            to = pl.ds(step * 16 * SKEW + z * SKEW, 8)
            qre[to, :] = re
            qim[to, :] = im

    left_half = lax.broadcasted_iota(jnp.int32, (8, LANES), 1) < PAIRS

    @pl.loop(0, 32, unroll=4)
    def _(step):
        plane = (step // 2) * PLANE
        skewed = (step // 2) * 32 * SKEW
        half = step % 2
        take = [
            pl.ds(skewed + (y // 8) * 16 * SKEW + half * 8 * SKEW + y % 8, 8, stride=SKEW) for y in range(NFFT)
        ]
        for y, (re, im) in enumerate(fft16([(qre[a, :], qim[a, :]) for a in take], -1)):
            at = pl.ds(pl.multiple_of(plane + y * NFFT + half * 8, 8), 8)
            vgrid[at, :] = jnp.where(left_half, re, pltpu.roll(im, PAIRS, 1))
            cgrid[at, :] = jnp.where(left_half, pltpu.roll(re, PAIRS, 1), im)

    fetch[2].wait()

    start = me * strip

    @pl.loop(0, strip // 32)
    def _(step):
        base = pl.multiple_of(step * 32, 32)
        got = [cgrid[pl.ds(idx_ref[start + base + u], 1), :] for u in range(32)]
        for u in range(32):
            cpick[pl.ds(base + u, 1), :] = got[u]

    fetch[6].wait()
    part = 2 * LANES

    def pick(first):
        for low in range(0, part, 32):
            got = [vgrid[pl.ds(idx_ref[first + low + u], 1), :] for u in range(32)]
            for u in range(32):
                vpick[pl.ds(first + low + u, 1), :] = got[u]

    def product(first):
        piece = vpick[pl.ds(first, part), :].astype(BF)
        return jnp.dot(w_ref[:, pl.ds(first, part)], piece, preferred_element_type=F32)

    pick(0)
    mixed[...] = jnp.zeros_like(mixed)

    @pl.loop(0, waves // part - 1)
    def _(step):
        first = pl.multiple_of(step * part, part)
        mixed[...] += product(first)
        pick(pl.multiple_of(first + part, part))

    screened = (mixed[...] + product(waves - part)).astype(BF)
    left = cpick[...].T.astype(BF)
    cross = jnp.dot(left, screened, preferred_element_type=F32)
    top, bottom = cross[:PAIRS], pltpu.roll(cross[PAIRS:], PAIRS, 1)
    lane = lax.broadcasted_iota(jnp.int32, (PAIRS, LANES), 1)
    total = jnp.where(lane < PAIRS, top + bottom, top - bottom)
    for d in range(width):
        blocks[d] = total[d * rows:(d + 1) * rows]
    copies = []
    for step in range(1, width):
        peer = lax.rem(me + step, width)
        copy = pltpu.make_async_remote_copy(
            src_ref=blocks.at[peer],
            dst_ref=slots.at[step - 1],
            send_sem=send_sem.at[step - 1],
            recv_sem=recv_sem.at[step - 1],
            device_id={"ga": peer},
            device_id_type=MESH,
        )
        copy.start()
        copies.append(copy)
    total = blocks[me]
    for step, copy in enumerate(copies):
        copy.wait_recv()
        total = total + slots[step]
    out_ref[...] = total
    for copy in ring + copies:
        copy.wait_send()


def body(band_coefs, screening, grid_index):
    width = lax.axis_size("ga")
    count = lax.axis_size("ka")
    strip, waves = screening.shape[1:]
    rows = PAIRS // width
    here = band_coefs[0]
    high, low, spread = (jnp.asarray(t) for t in tables())
    hbm = pl.BlockSpec(memory_space=pltpu.HBM)
    result = pl.pallas_call(
        functools.partial(compute, width, count, strip, rows),
        out_shape=jax.ShapeDtypeStruct((rows, LANES), F32),
        in_specs=[hbm] * 7,
        out_specs=pl.BlockSpec(memory_space=pltpu.VMEM),
        scratch_shapes=[
            pltpu.VMEM(here.shape, BF),
            pltpu.VMEM(here.shape, BF),
            pltpu.VMEM((1, waves), jnp.int32),
            pltpu.SMEM((waves,), jnp.int32),
            pltpu.VMEM((strip, waves), BF),
            pltpu.VMEM(high.shape, BF),
            pltpu.VMEM(low.shape, BF),
            pltpu.VMEM(spread.shape, BF),
            pltpu.VMEM((GRID, LANES), F32),
            pltpu.VMEM((GRID, LANES), F32),
            pltpu.VMEM((2 * PLANE, LANES), F32),
            pltpu.VMEM((2 * PLANE, LANES), F32),
            pltpu.VMEM((32 * 16 * SKEW, LANES), F32),
            pltpu.VMEM((32 * 16 * SKEW, LANES), F32),
            pltpu.VMEM((GRID, LANES), F32),
            pltpu.VMEM((GRID, LANES), F32),
            pltpu.VMEM((waves, LANES), F32),
            pltpu.VMEM((strip, LANES), F32),
            pltpu.VMEM((strip, LANES), F32),
            pltpu.VMEM((width, rows, LANES), F32),
            pltpu.VMEM((width - 1, rows, LANES), F32),
            pltpu.SemaphoreType.DMA((7,)),
            pltpu.SemaphoreType.DMA((4,)),
            pltpu.SemaphoreType.DMA((4,)),
            pltpu.SemaphoreType.DMA((width - 1,)),
            pltpu.SemaphoreType.DMA((width - 1,)),
        ],
        compiler_params=pltpu.CompilerParams(
            collective_id=0, has_side_effects=True, vmem_limit_bytes=56 * 1024 * 1024
        ),
    )(here, grid_index[None], grid_index, screening[0], high, low, spread)
    return (result * (1.0 / math.sqrt(waves)))[None, None]


def solution(mesh):
    return jax.shard_map(
        body,
        mesh=mesh,
        in_specs=(P("ka", None, None, None), P(None, "ga", None), P()),
        out_specs=P("ka", None, "ga", None),
        check_vma=False,
    )
```
